32 devices in a mesh: region: 2 (over y), member: 16 (over z, x, core).
Axes of the slice: x: 2, y: 2, z: 4, core: 2. Of those that a mesh axis runs over, the one named last changes fastest.
Arguments:
- perm_prior: float32 [128, 64, 512], P(('region', 'member')), parts along dimension 0, may hold values from -1.5 to 1.5
- start_height: float32 [128, 512], P('region'), parts along dimension 0, may hold values from 0.2 to 1
- top_surface: float32 [128, 512], P('region'), parts along dimension 0, may hold values from 0 to 0.5
- porosity: float32 [128, 512], P('region'), parts along dimension 0, may hold values from 0.15 to 0.3
- well_mask: int32 [128, 512], P('region'), parts along dimension 0, may hold values 0 or 1
- obs_cells: int32 [4, 128], P('region'), parts along dimension 0, may hold values from 0 to 32767
- observed: float32 [4, 128], P('region'), parts along dimension 0, may hold values from -0.3 to 0.3
- obs_error: float32 [256], P('region'), parts along dimension 0, may hold values from 0.03 to 0.06
- noise_table: int32 [4, 64, 128], P('region', 'member'), parts along dimension 0, may hold values from 0 to 255
Outputs:
- perm_post: float32 [128, 64, 512], P(('region', 'member')), parts along dimension 0
The draws below stay inside these ranges and needn't reach their ends.
There are 2 independent parts, one for each index of `region`. The reference program is written for one: setup_inputs(seed, part) draws one part's arguments, and reference() takes and returns one part's arrays. A program takes and returns all parts, laid end to end along the dimension named above; each array names one. Nothing has to cross between parts.
All inputs are finite; a program needn't handle non-finite values.
Results may differ from the reference program's by a relative error of at most 0.00029.
Values sent between devices are 32-bit elements; how exact they have to be, the bound alone decides.
A program may use at most 128 MiB of HBM per device.

```python
import math
import jax
import jax.numpy as jnp
from jax import lax

NR = 64
NC = 512
MEM_DEV = 4
STEPS = 3
CYCLES = 2
M = 64
NOBS = 128


def set_ends(drawn, key, least, high):
    place = [jax.random.randint(jax.random.fold_in(key, axis), (), 0, length) for axis, length in enumerate(drawn.shape)]
    longest = drawn.shape.index(max(drawn.shape))
    neighbour = place[:longest] + [(place[longest] + 1) % drawn.shape[longest]] + place[longest + 1:]
    return drawn.at[tuple(place)].set(least).at[tuple(neighbour)].set(high)


def level_of(stream_key, shape, split, low, largest):
    def one(axis_at, shards_of):
        steps = jax.random.uniform(jax.random.fold_in(jax.random.fold_in(stream_key, 6), axis_at), (shards_of,), jnp.float32, low / len(split), largest / len(split))
        return jnp.repeat(jnp.exp(steps), shape[axis_at] // shards_of).reshape((-1,) + (1,) * (len(shape) - axis_at - 1))

    level = one(*split[0])
    for cut in split[1:]:
        level = level * one(*cut)
    return level


def bell_draw(rng, shape, spread, bound, pieces=(), kind=jnp.bfloat16):
    values = spread * jax.random.normal(rng, shape, jnp.float32)
    if pieces:
        values = values * level_of(rng, shape, pieces, -0.22, 0.18)
    return jnp.clip(values, -bound, bound).astype(kind)


def setup_inputs(seed: int = 0, part: int = 0) -> dict:
    key_list = jax.random.split(jax.random.key(seed), 10)
    own_keys = jax.random.split(jax.random.fold_in(key_list[9], part), 10)
    return {
        "perm_prior": bell_draw(own_keys[0], (M, NR, NC), 0.5, 1.5, ((0, 16),), jnp.float32),
        "start_height": jnp.clip(jax.random.uniform(own_keys[1], (NR, NC), jnp.float32, 0.2, 1.0), 0.2, 1.0),
        "top_surface": jnp.clip(jax.random.uniform(own_keys[2], (NR, NC), jnp.float32, 0.0, 0.5), 0.0, 0.5),
        "porosity": jnp.clip(jax.random.uniform(own_keys[3], (NR, NC), jnp.float32, 0.15, 0.3), 0.15, 0.3),
        "well_mask": set_ends((jax.random.randint(own_keys[4], (NR, NC), 0, 64) < 1).astype(jnp.int32), jax.random.fold_in(own_keys[4], 1), 0, 1),
        "obs_cells": set_ends(jax.random.randint(own_keys[5], (CYCLES, NOBS), 0, NR * NC), jax.random.fold_in(own_keys[5], 1), 0, (NR * NC) - 1).astype(jnp.int32),
        "observed": bell_draw(own_keys[6], (CYCLES, NOBS), 0.05, 0.3, (), jnp.float32),
        "obs_error": jnp.clip(jnp.exp(jax.random.uniform(own_keys[7], (NOBS,), jnp.float32, math.log(0.03), math.log(0.06))), 0.03, 0.06),
        "noise_table": set_ends(jax.random.randint(own_keys[8], (CYCLES, M, NOBS), 0, 256), jax.random.fold_in(own_keys[8], 1), 0, 255).astype(jnp.int32),
    }


TIME_STEP = 0.01
INJECT_RATE = 1.0
INFLATION = 2.0
NOISE_CENTER = 127.5
NOISE_SPREAD = 73.9

def harmonic(first, second):
    return 2.0 * first * second / (first + second)

def plume_steps(perm_log, start_height, top_surface, porosity, well_mask):
    conduct = jnp.exp(perm_log)
    trans_rows = harmonic(conduct[:, :-1, :], conduct[:, 1:, :])
    trans_cols = harmonic(conduct[:, :, :-1], conduct[:, :, 1:])
    source = INJECT_RATE * well_mask.astype(jnp.float32)
    factor = TIME_STEP / porosity
    height = jnp.broadcast_to(start_height, perm_log.shape)
    for step_index in range(STEPS):
        level = height + top_surface
        flux_rows = trans_rows * 0.5 * (height[:, :-1, :] + height[:, 1:, :]) * (level[:, :-1, :] - level[:, 1:, :])
        flux_cols = trans_cols * 0.5 * (height[:, :, :-1] + height[:, :, 1:]) * (level[:, :, :-1] - level[:, :, 1:])
        inflow = jnp.pad(flux_rows, ((0, 0), (1, 0), (0, 0))) - jnp.pad(flux_rows, ((0, 0), (0, 1), (0, 0)))
        inflow = inflow + jnp.pad(flux_cols, ((0, 0), (0, 0), (1, 0))) - jnp.pad(flux_cols, ((0, 0), (0, 0), (0, 1)))
        height = height + factor * (inflow + source)
    return height

def make_innovation(predicted, observed, obs_error, noise):
    perturb = (noise.astype(jnp.float32) - NOISE_CENTER) / NOISE_SPREAD
    return (observed + math.sqrt(INFLATION) * obs_error * perturb - predicted) / obs_error

def gram_terms(predicted, innovation, obs_error):
    members = predicted.shape[0]
    scaled = (predicted - lax.optimization_barrier(jnp.mean(predicted, axis=0, keepdims=True))) / (obs_error * math.sqrt(members - 1.0))
    dims = (((1,), (1,)), ((), ()))
    gram = lax.dot_general(scaled, scaled, dims, precision=lax.Precision.HIGHEST)
    cross = lax.dot_general(scaled, innovation, dims, precision=lax.Precision.HIGHEST)
    return (gram, cross)

def solve_weights(gram, cross):
    members = gram.shape[0]
    full = gram + INFLATION * jnp.eye(members, dtype=jnp.float32)
    factor = jnp.linalg.cholesky(full)
    return jax.scipy.linalg.cho_solve((factor, True), cross)

def mix_fields(fields, weights):
    members = fields.shape[0]
    anomaly = (fields - lax.optimization_barrier(jnp.mean(fields, axis=0, keepdims=True))) / math.sqrt(members - 1.0)
    return fields + lax.dot_general(weights, anomaly, (((0,), (0,)), ((), ())), precision=lax.Precision.HIGHEST)

def reference(perm_prior, start_height, top_surface, porosity, well_mask, obs_cells, observed, obs_error, noise_table):
    members = perm_prior.shape[0]
    perm = perm_prior
    for cycle_index in range(CYCLES):
        cells = obs_cells[cycle_index]
        blocks = perm.reshape(members // MEM_DEV, MEM_DEV, NR, NC)

        def predict_block(block):
            height = plume_steps(block, start_height, top_surface, porosity, well_mask)
            return jnp.take((height - start_height).reshape(MEM_DEV, NR * NC), cells, axis=1)
        predicted = lax.map(predict_block, blocks).reshape(members, NOBS)
        innovation = make_innovation(predicted, observed[cycle_index], obs_error, noise_table[cycle_index])
        gram, cross = gram_terms(predicted, innovation, obs_error)
        weights = solve_weights(gram, cross)
        perm = mix_fields(perm.reshape(members, NR * NC), weights).reshape(members, NR, NC)
    return perm
```

```python
import functools
import math

import jax
import jax.numpy as jnp
from jax import lax
from jax.experimental import pallas as pl
from jax.experimental.pallas import tpu as pltpu
from jax.sharding import PartitionSpec as P

MESH = pl.DeviceIdType.MESH
HIGHEST = lax.Precision.HIGHEST
SIDE = 8
PATCH = SIDE * SIDE
LANES = 128
PAIR = LANES // PATCH
FIELDS = 8

STEPS = 3
CYCLES = 2


TIME_STEP = 0.01
INJECT_RATE = 1.0
INFLATION = 2.0
NOISE_CENTER = 127.5
NOISE_SPREAD = 73.9


def harmonic(first, second):
    return 2.0 * first * second / (first + second)


def plume_steps(perm_log, start_height, top_surface, porosity, well_mask):
    conduct = jnp.exp(perm_log)
    trans_rows = harmonic(conduct[:, :-1, :], conduct[:, 1:, :])
    trans_cols = harmonic(conduct[:, :, :-1], conduct[:, :, 1:])
    source = INJECT_RATE * well_mask.astype(jnp.float32)
    factor = TIME_STEP / porosity
    height = jnp.broadcast_to(start_height, perm_log.shape)
    for step_index in range(STEPS):
        level = height + top_surface
        flux_rows = (
            trans_rows
            * 0.5
            * (height[:, :-1, :] + height[:, 1:, :])
            * (level[:, :-1, :] - level[:, 1:, :])
        )
        flux_cols = (
            trans_cols
            * 0.5
            * (height[:, :, :-1] + height[:, :, 1:])
            * (level[:, :, :-1] - level[:, :, 1:])
        )
        inflow = jnp.pad(flux_rows, ((0, 0), (1, 0), (0, 0))) - jnp.pad(
            flux_rows, ((0, 0), (0, 1), (0, 0))
        )
        inflow = (
            inflow
            + jnp.pad(flux_cols, ((0, 0), (0, 0), (1, 0)))
            - jnp.pad(flux_cols, ((0, 0), (0, 0), (0, 1)))
        )
        height = height + factor * (inflow + source)
    return height


def make_innovation(predicted, observed, obs_error, noise):
    perturb = (noise.astype(jnp.float32) - NOISE_CENTER) / NOISE_SPREAD
    return (observed + math.sqrt(INFLATION) * obs_error * perturb - predicted) / obs_error


def gram_terms(predicted, innovation, obs_error):
    members = predicted.shape[0]
    scaled = (predicted - jnp.mean(predicted, axis=0, keepdims=True)) / (
        obs_error * math.sqrt(members - 1.0)
    )
    dims = (((1,), (1,)), ((), ()))
    gram = lax.dot_general(scaled, scaled, dims, precision=lax.Precision.HIGHEST)
    cross = lax.dot_general(scaled, innovation, dims, precision=lax.Precision.HIGHEST)
    return (gram, cross)


def solve_weights(gram, cross):
    members = gram.shape[0]
    full = gram + INFLATION * jnp.eye(members, dtype=jnp.float32)
    factor = jnp.linalg.cholesky(full)
    return jax.scipy.linalg.cho_solve((factor, True), cross)


def mix_fields(fields, weights):
    members = fields.shape[0]
    anomaly = (fields - jnp.mean(fields, axis=0, keepdims=True)) / math.sqrt(members - 1.0)
    return fields + lax.dot_general(
        weights, anomaly, (((0,), (0,)), ((), ())), precision=lax.Precision.HIGHEST
    )


def ensemble_solve(predicted, innovation, obs_error):
    whole_pred, whole_innov = (
        lax.all_gather(predicted, "member", axis=0, tiled=True),
        lax.all_gather(innovation, "member", axis=0, tiled=True),
    )
    gram, cross = gram_terms(whole_pred, whole_innov, obs_error)
    return solve_weights(gram, cross)


def on_device(
    perm_prior,
    start_height,
    top_surface,
    porosity,
    well_mask,
    obs_cells,
    observed,
    obs_error,
    noise_table,
):
    held_count, map_rows, map_cols = perm_prior.shape
    perm = perm_prior
    for cycle_index in range(CYCLES):
        height = plume_steps(perm, start_height, top_surface, porosity, well_mask)
        change = (height - start_height).reshape(held_count, map_rows * map_cols)
        predicted = jnp.take(change, obs_cells[cycle_index], axis=1)
        innovation = make_innovation(
            predicted, observed[cycle_index], obs_error, noise_table[cycle_index]
        )
        weights = ensemble_solve(predicted, innovation, obs_error)
        cell_major = lax.all_to_all(
            perm.reshape(held_count, map_rows * map_cols),
            "member",
            split_axis=1,
            concat_axis=0,
            tiled=True,
        )
        cell_major = mix_fields(cell_major, weights)
        returned = lax.all_to_all(cell_major, "member", split_axis=0, concat_axis=1, tiled=True)
        perm = returned.reshape(held_count, map_rows, map_cols)
    return perm


def patch_plume(perm_log, start, top, porosity, well):
    axis = perm_log.ndim - 1
    lane = lax.broadcasted_iota(jnp.int32, perm_log.shape, axis)
    inner_col = (lane % SIDE) < SIDE - 1
    inner_row = (lane % PATCH) < PATCH - SIDE

    def ahead(x, by):
        return pltpu.roll(x, LANES - by, axis)

    def behind(x, by):
        return pltpu.roll(x, by, axis)

    conduct = jnp.exp(perm_log)
    half_cols = jnp.where(inner_col, 0.5 * harmonic(conduct, ahead(conduct, 1)), 0.0)
    half_rows = jnp.where(inner_row, 0.5 * harmonic(conduct, ahead(conduct, SIDE)), 0.0)
    source = INJECT_RATE * well
    factor = TIME_STEP / porosity
    begin = jnp.broadcast_to(start, perm_log.shape)
    height = begin
    for _ in range(STEPS):
        level = height + top
        flux_cols = half_cols * (height + ahead(height, 1)) * (level - ahead(level, 1))
        flux_rows = half_rows * (height + ahead(height, SIDE)) * (level - ahead(level, SIDE))
        inflow = behind(flux_cols, 1) - flux_cols + behind(flux_rows, SIDE) - flux_rows
        height = height + factor * (inflow + source)
    return height - begin


def local_kernel(
    cells_ref,
    perm_ref,
    start_ref,
    top_ref,
    porosity_ref,
    well_ref,
    observed_ref,
    error_ref,
    noise_ref,
    first_ref,
    patch_ref,
    mark_ref,
    stack,
    patch_one,
    mark_one,
):
    held, rows, cols = perm_ref.shape
    nobs = observed_ref.shape[1]
    for strip in range(cols // LANES):
        across = slice(strip * LANES, (strip + 1) * LANES)
        fields = [perm_ref[member, :, across] for member in range(held)]
        fields += [start_ref[:, across], top_ref[:, across], porosity_ref[:, across]]
        fields += [well_ref[:, across].astype(jnp.float32)]
        for index, field in enumerate(fields):
            stack[strip, pl.ds(index, rows, stride=FIELDS), :] = field

    lane = lax.broadcasted_iota(jnp.int32, (FIELDS, LANES), 1)

    for cycle in range(CYCLES):
        patches, marks = (patch_one, mark_one) if cycle == 0 else (patch_ref, mark_ref)

        @functools.partial(lax.fori_loop, 0, nobs // PAIR, init_val=0, unroll=4)
        def _(chunk, carry):
            total = jnp.zeros((FIELDS, LANES), jnp.float32)
            mark = jnp.zeros((FIELDS, LANES), jnp.float32)
            for part in range(PAIR):
                cell = cells_ref[cycle, chunk * PAIR + part]
                row, col = lax.div(cell, cols), lax.rem(cell, cols)
                row0 = jnp.clip(row - STEPS, 0, rows - SIDE)
                col0 = jnp.clip(col - STEPS, 0, cols - SIDE)
                low = lax.div(col0, LANES)
                high = jnp.minimum(low + 1, cols // LANES - 1)
                within = col0 - low * LANES
                for i in range(SIDE):
                    at = pl.multiple_of((row0 + i) * FIELDS, FIELDS)
                    left = stack[low, pl.ds(at, FIELDS), :]
                    right = stack[high, pl.ds(at, FIELDS), :]
                    window = jnp.where(lane >= within, left, right)
                    place = part * PATCH + i * SIDE
                    moved = pltpu.roll(window, lax.rem(place + LANES - within, LANES), 1)
                    total = jnp.where((lane >= place) & (lane < place + SIDE), moved, total)
                spot = part * PATCH + (row - row0) * SIDE + (col - col0)
                mark = jnp.where(lane == spot, 1.0, mark)
            patches[chunk] = total
            marks[chunk] = mark
            return carry

    group = 8
    wide = lax.broadcasted_iota(jnp.int32, (group, held, LANES), 2)
    turn = lax.broadcasted_iota(jnp.int32, (group, held, LANES), 0)

    def run(index, acc):
        at = pl.ds(index * group, group)
        change = patch_plume(
            patch_one[at, 0:held, :],
            patch_one[at, held : held + 1, :],
            patch_one[at, held + 1 : held + 2, :],
            patch_one[at, held + 2 : held + 3, :],
            patch_one[at, held + 3 : held + 4, :],
        )
        change = change * mark_one[at, 0:held, :]
        for part in range(PAIR):
            here = (wide >= part * PATCH) & (wide < (part + 1) * PATCH)
            sums = jnp.sum(jnp.where(here, change, 0.0), axis=2, keepdims=True)
            slot = (index * group + turn) * PAIR + part
            acc = acc + jnp.sum(jnp.where(wide == slot, sums, 0.0), axis=0)
        return acc

    predicted = lax.fori_loop(
        0, nobs // (PAIR * group), run, jnp.zeros((held, nobs), jnp.float32)
    )
    error = error_ref[...]
    first_ref[0:held, :] = predicted
    first_ref[held : 2 * held, :] = make_innovation(
        predicted, observed_ref[0:1, :], error, noise_ref[0]
    )
    first_ref[2 * held : 3 * held, :] = make_innovation(
        jnp.zeros_like(predicted), observed_ref[1:2, :], error, noise_ref[1]
    )
    first_ref[3 * held : 4 * held, :] = jnp.zeros_like(predicted)


def dot(a, b, dims):
    return lax.dot_general(
        a, b, (dims, ((), ())), precision=HIGHEST, preferred_element_type=jnp.float32
    )


def eliminate(gram, cross):
    size = gram.shape[0]
    work = jnp.concatenate([gram, cross], axis=1)
    line = lax.broadcasted_iota(jnp.int32, work.shape, 0)
    for k in range(size):
        row = work[k : k + 1, :] * (1.0 / work[k : k + 1, k : k + 1])
        work = jnp.where(line == k, row, work - work[:, k : k + 1] * row)
    return work[:, size:]


def add_inflation(gram):
    one = lax.broadcasted_iota(jnp.int32, gram.shape, 0)
    two = lax.broadcasted_iota(jnp.int32, gram.shape, 1)
    return jnp.where(one == two, gram + INFLATION, gram)


def mix(fields, weights):
    members = fields.shape[0]
    anomaly = (fields - jnp.mean(fields, axis=0, keepdims=True)) / math.sqrt(members - 1.0)
    return fields + dot(weights, anomaly, ((0,), (0,)))


def ensemble_kernel(
    count,
    perm_ref,
    first_ref,
    patch_ref,
    mark_ref,
    error_ref,
    error_col_ref,
    out_ref,
    first_all,
    patch_all,
    pred_all,
    block,
    mixed,
    send_sem,
    recv_sem,
    local_sem,
):
    held, rows, cols = perm_ref.shape
    members = held * count
    nobs = error_ref.shape[1]
    own_obs = nobs // count
    own_chunks = own_obs // PAIR
    me = lax.axis_index("member")
    _, tall, wide = block.shape
    across = cols // wide

    def cells_of(ref, device):
        return ref.at[
            :,
            pl.ds(pl.multiple_of((device // across) * tall, tall), tall),
            pl.ds(pl.multiple_of((device % across) * wide, wide), wide),
        ]

    def members_of(ref, device):
        return ref.at[pl.ds(device * held, held)]

    def obs_of(ref, device):
        return ref.at[pl.ds(pl.multiple_of(device * own_obs, own_obs), own_obs)]

    def chunks_of(ref, device):
        return ref.at[pl.ds(device * own_chunks, own_chunks)]

    ways = [
        (lambda peer: first_ref, lambda owner: first_all.at[owner]),
        (lambda peer: chunks_of(patch_ref, peer), lambda owner: patch_all.at[owner]),
        (lambda peer: cells_of(perm_ref, peer), lambda owner: members_of(block, owner)),
        (lambda peer: obs_of(pred_all, me), lambda owner: obs_of(pred_all, owner)),
        (lambda peer: members_of(mixed, peer), lambda owner: cells_of(out_ref, owner)),
    ]

    def transfer(kind, peer, owner, slot):
        source, target = ways[kind]
        return pltpu.make_async_remote_copy(
            src_ref=source(peer),
            dst_ref=target(owner),
            send_sem=send_sem.at[kind, slot],
            recv_sem=recv_sem.at[kind, slot],
            device_id={"member": peer},
            device_id_type=MESH,
        )

    def each(body):
        def step(j, carry):
            body(j)
            return carry

        lax.fori_loop(1, count, step, 0)

    def send(kind):
        each(lambda j: transfer(kind, lax.rem(me + j, count), me, j).start())

    def receive(kind):
        each(lambda j: transfer(kind, me, lax.rem(me + count - j, count), j).wait_recv())

    def sent(kind):
        each(lambda j: transfer(kind, lax.rem(me + j, count), me, j).wait_send())

    barrier = pltpu.get_barrier_semaphore()
    each(
        lambda j: pl.semaphore_signal(
            barrier,
            inc=1,
            device_id={"member": lax.rem(me + j, count)},
            device_id_type=MESH,
        )
    )
    pl.semaphore_wait(barrier, count - 1)

    send(0)
    send(1)
    send(2)
    own_in = pltpu.make_async_copy(cells_of(perm_ref, me), members_of(block, me), local_sem.at[0])
    own_in.start()
    first_all[me] = first_ref[...]
    patch_all[me] = patch_ref[pl.ds(me * own_chunks, own_chunks)]

    depth = first_ref.shape[0]
    line = lax.broadcasted_iota(jnp.int32, (members, count * depth), 0)
    spot = lax.broadcasted_iota(jnp.int32, (members, count * depth), 1)
    home = (line // held) * depth + line % held

    def pick(whole, offset):
        return dot(jnp.where(spot == home + offset, 1.0, 0.0), whole, ((1,), (0,)))

    error = error_ref[...]
    root = math.sqrt(members - 1.0)

    receive(0)
    whole = first_all[...].reshape(count * depth, nobs)
    predicted = pick(whole, 0)
    innovation = pick(whole, held)
    base = pick(whole, 2 * held)
    scaled = (predicted - jnp.mean(predicted, axis=0, keepdims=True)) / (error * root)
    both = dot(scaled, jnp.concatenate([scaled, innovation], axis=0), ((1,), (1,)))
    first_weights = eliminate(add_inflation(both[:, :members]), both[:, members:])

    receive(1)
    line2 = lax.broadcasted_iota(jnp.int32, (members, count * FIELDS), 0)
    spot2 = lax.broadcasted_iota(jnp.int32, (members, count * FIELDS), 1)
    choose = jnp.where(spot2 == (line2 // held) * FIELDS + line2 % held, 1.0, 0.0)
    fresh = jnp.zeros((own_obs, members), jnp.float32)
    one = lax.broadcasted_iota(jnp.int32, (own_obs, LANES), 0)
    two = lax.broadcasted_iota(jnp.int32, (own_obs, LANES), 1)
    for q in range(own_chunks):
        at = me * own_chunks + q
        values = patch_all[:, q].reshape(count * FIELDS, LANES)
        prior = dot(choose, values, ((1,), (0,)))
        change = patch_plume(
            mix(prior, first_weights),
            patch_ref[at, held : held + 1, :],
            patch_ref[at, held + 1 : held + 2, :],
            patch_ref[at, held + 2 : held + 3, :],
            patch_ref[at, held + 3 : held + 4, :],
        )
        change = change * mark_ref[at, 0:1, :]
        ones = jnp.where(two // PATCH + q * PAIR == one, 1.0, 0.0)
        fresh = fresh + dot(ones, change, ((1,), (1,)))
    pred_all[pl.ds(pl.multiple_of(me * own_obs, own_obs), own_obs), 0:members] = fresh
    pred_all[pl.ds(pl.multiple_of(me * own_obs, own_obs), own_obs), members:] = jnp.zeros(
        (own_obs, pred_all.shape[1] - members), jnp.float32
    )
    send(3)

    receive(2)
    own_in.wait()
    for r in range(tall):
        mixed[:, r, :] = mix(block[:, r, :], first_weights)

    receive(3)
    table = pred_all[:, 0:members]
    error_col = error_col_ref[:, 0:1]
    scaled2 = (table - jnp.mean(table, axis=1, keepdims=True)) / (error_col * root)
    gram = dot(scaled2, scaled2, ((0,), (0,)))
    cross = dot(scaled2, base, ((0,), (1,))) - dot(scaled2, table / error_col, ((0,), (0,)))
    second_weights = eliminate(add_inflation(gram), cross)
    for r in range(tall):
        mixed[:, r, :] = mix(mixed[:, r, :], second_weights)
    send(4)
    own_out = pltpu.make_async_copy(members_of(mixed, me), cells_of(out_ref, me), local_sem.at[1])
    own_out.start()
    for kind in range(4):
        sent(kind)
    own_out.wait()
    receive(4)
    sent(4)


def patch_device(count, perm, start, top, porosity, well, cells, observed, error, noise):
    held, rows, cols = perm.shape
    nobs = observed.shape[1]
    members = held * count
    chunks = nobs // PAIR
    vmem = pl.BlockSpec(memory_space=pltpu.VMEM)
    first, patch, mark = pl.pallas_call(
        local_kernel,
        out_shape=[
            jax.ShapeDtypeStruct((4 * held, nobs), jnp.float32),
            jax.ShapeDtypeStruct((chunks, FIELDS, LANES), jnp.float32),
            jax.ShapeDtypeStruct((chunks, FIELDS, LANES), jnp.float32),
        ],
        in_specs=[pl.BlockSpec(memory_space=pltpu.SMEM)] + [vmem] * 8,
        out_specs=[vmem] * 3,
        scratch_shapes=[
            pltpu.VMEM((cols // LANES, rows * FIELDS, LANES), jnp.float32),
            pltpu.VMEM((chunks, FIELDS, LANES), jnp.float32),
            pltpu.VMEM((chunks, FIELDS, LANES), jnp.float32),
        ],
        compiler_params=pltpu.CompilerParams(vmem_limit_bytes=32 * 1024 * 1024),
    )(cells, perm, start, top, porosity, well, observed, error.reshape(1, nobs), noise)
    across = (count * SIDE) // rows
    wide = cols // across
    kinds = 5
    return pl.pallas_call(
        functools.partial(ensemble_kernel, count),
        out_shape=jax.ShapeDtypeStruct(perm.shape, jnp.float32),
        in_specs=[vmem] * 6,
        out_specs=vmem,
        scratch_shapes=[
            pltpu.VMEM((count, 4 * held, nobs), jnp.float32),
            pltpu.VMEM((count, chunks // count, FIELDS, LANES), jnp.float32),
            pltpu.VMEM((nobs, LANES), jnp.float32),
            pltpu.VMEM((members, SIDE, wide), jnp.float32),
            pltpu.VMEM((members, SIDE, wide), jnp.float32),
            pltpu.SemaphoreType.DMA((kinds, count)),
            pltpu.SemaphoreType.DMA((kinds, count)),
            pltpu.SemaphoreType.DMA((2,)),
        ],
        compiler_params=pltpu.CompilerParams(
            collective_id=0, has_side_effects=True, vmem_limit_bytes=32 * 1024 * 1024
        ),
    )(
        perm,
        first,
        patch,
        mark,
        error.reshape(1, nobs),
        jnp.broadcast_to(error.reshape(nobs, 1), (nobs, LANES)),
    )


def fits(count, held, rows, cols, nobs):
    members, own_obs = count * held, nobs // count
    return (
        held == FIELDS // 2
        and members <= LANES // 2
        and nobs == LANES
        and nobs == own_obs * count
        and own_obs % 8 == 0
        and rows % SIDE == 0
        and (count * SIDE) % rows == 0
        and cols % ((count * SIDE // rows) * LANES) == 0
    )


def device_program(perm, *rest):
    count = lax.axis_size("member")
    held, rows, cols = perm.shape
    if fits(count, held, rows, cols, rest[5].shape[1]):
        return patch_device(count, perm, *rest)
    return on_device(perm, *rest)


def solution(mesh):
    return jax.shard_map(
        device_program,
        mesh=mesh,
        in_specs=(
            P(("region", "member"), None, None),
            P("region", None),
            P("region", None),
            P("region", None),
            P("region", None),
            P("region", None),
            P("region", None),
            P("region"),
            P("region", "member", None),
        ),
        out_specs=P(("region", "member"), None, None),
        check_vma=False,
    )
```

```python
import functools
import math

import jax
import jax.numpy as jnp
from jax import lax
from jax.experimental import pallas as pl
from jax.experimental.pallas import tpu as pltpu
from jax.sharding import PartitionSpec as P

MESH = pl.DeviceIdType.MESH
HIGHEST = lax.Precision.HIGHEST
SIDE = 8
LANES = 128
HALF = LANES // 2
QUARTERS = SIDE // 2
FIELDS = 8
SUBLANES = 8
KINDS = 5

STEPS = 3
CYCLES = 2


TIME_STEP = 0.01
INJECT_RATE = 1.0
INFLATION = 2.0
NOISE_CENTER = 127.5
NOISE_SPREAD = 73.9


def harmonic(first, second):
    return 2.0 * first * second / (first + second)


def plume_steps(perm_log, start_height, top_surface, porosity, well_mask):
    conduct = jnp.exp(perm_log)
    trans_rows = harmonic(conduct[:, :-1, :], conduct[:, 1:, :])
    trans_cols = harmonic(conduct[:, :, :-1], conduct[:, :, 1:])
    source = INJECT_RATE * well_mask.astype(jnp.float32)
    factor = TIME_STEP / porosity
    height = jnp.broadcast_to(start_height, perm_log.shape)
    for step_index in range(STEPS):
        level = height + top_surface
        flux_rows = (
            trans_rows
            * 0.5
            * (height[:, :-1, :] + height[:, 1:, :])
            * (level[:, :-1, :] - level[:, 1:, :])
        )
        flux_cols = (
            trans_cols
            * 0.5
            * (height[:, :, :-1] + height[:, :, 1:])
            * (level[:, :, :-1] - level[:, :, 1:])
        )
        inflow = jnp.pad(flux_rows, ((0, 0), (1, 0), (0, 0))) - jnp.pad(
            flux_rows, ((0, 0), (0, 1), (0, 0))
        )
        inflow = (
            inflow
            + jnp.pad(flux_cols, ((0, 0), (0, 0), (1, 0)))
            - jnp.pad(flux_cols, ((0, 0), (0, 0), (0, 1)))
        )
        height = height + factor * (inflow + source)
    return height


def make_innovation(predicted, observed, obs_error, noise):
    perturb = (noise.astype(jnp.float32) - NOISE_CENTER) / NOISE_SPREAD
    return (observed + math.sqrt(INFLATION) * obs_error * perturb - predicted) / obs_error


def gram_terms(predicted, innovation, obs_error):
    members = predicted.shape[0]
    scaled = (predicted - jnp.mean(predicted, axis=0, keepdims=True)) / (
        obs_error * math.sqrt(members - 1.0)
    )
    dims = (((1,), (1,)), ((), ()))
    gram = lax.dot_general(scaled, scaled, dims, precision=lax.Precision.HIGHEST)
    cross = lax.dot_general(scaled, innovation, dims, precision=lax.Precision.HIGHEST)
    return (gram, cross)


def solve_weights(gram, cross):
    members = gram.shape[0]
    full = gram + INFLATION * jnp.eye(members, dtype=jnp.float32)
    factor = jnp.linalg.cholesky(full)
    return jax.scipy.linalg.cho_solve((factor, True), cross)


def mix_fields(fields, weights):
    members = fields.shape[0]
    anomaly = (fields - jnp.mean(fields, axis=0, keepdims=True)) / math.sqrt(members - 1.0)
    return fields + lax.dot_general(
        weights, anomaly, (((0,), (0,)), ((), ())), precision=lax.Precision.HIGHEST
    )


def ensemble_solve(predicted, innovation, obs_error):
    whole_pred, whole_innov = (
        lax.all_gather(predicted, "member", axis=0, tiled=True),
        lax.all_gather(innovation, "member", axis=0, tiled=True),
    )
    gram, cross = gram_terms(whole_pred, whole_innov, obs_error)
    return solve_weights(gram, cross)


def on_device(
    perm_prior,
    start_height,
    top_surface,
    porosity,
    well_mask,
    obs_cells,
    observed,
    obs_error,
    noise_table,
):
    held_count, map_rows, map_cols = perm_prior.shape
    perm = perm_prior
    for cycle_index in range(CYCLES):
        height = plume_steps(perm, start_height, top_surface, porosity, well_mask)
        change = (height - start_height).reshape(held_count, map_rows * map_cols)
        predicted = jnp.take(change, obs_cells[cycle_index], axis=1)
        innovation = make_innovation(
            predicted, observed[cycle_index], obs_error, noise_table[cycle_index]
        )
        weights = ensemble_solve(predicted, innovation, obs_error)
        cell_major = lax.all_to_all(
            perm.reshape(held_count, map_rows * map_cols),
            "member",
            split_axis=1,
            concat_axis=0,
            tiled=True,
        )
        cell_major = mix_fields(cell_major, weights)
        returned = lax.all_to_all(cell_major, "member", split_axis=0, concat_axis=1, tiled=True)
        perm = returned.reshape(held_count, map_rows, map_cols)
    return perm


def patch_plume(perm_log, start, top, porosity, well):
    axis = perm_log[0].ndim - 1
    lane = lax.broadcasted_iota(jnp.int32, perm_log[0].shape, axis)
    inner_col = (lane % SIDE) < SIDE - 1
    upper = lane < HALF

    def right_of(x):
        return pltpu.roll(x, LANES - 1, axis)

    def left_of(x):
        return pltpu.roll(x, 1, axis)

    def below(xs):
        return xs[1:] + [pltpu.roll(xs[0], HALF, axis)]

    def above(xs):
        return [pltpu.roll(xs[-1], HALF, axis)] + xs[:-1]

    last = QUARTERS - 1
    conduct = [jnp.exp(p) for p in perm_log]
    half_cols = [jnp.where(inner_col, 0.5 * harmonic(c, right_of(c)), 0.0) for c in conduct]
    half_rows = [0.5 * harmonic(c, d) for c, d in zip(conduct, below(conduct))]
    half_rows[last] = jnp.where(upper, half_rows[last], 0.0)
    factor = [TIME_STEP / p for p in porosity]
    gain = [INJECT_RATE * w for w in well]
    begin = [jnp.broadcast_to(s, p.shape) for s, p in zip(start, perm_log)]
    height = begin
    for _ in range(STEPS):
        level = [h + t for h, t in zip(height, top)]
        flux_cols = [
            k * (h + right_of(h)) * (s - right_of(s))
            for k, h, s in zip(half_cols, height, level)
        ]
        flux_rows = [
            k * (h + g) * (s - r)
            for k, h, g, s, r in zip(half_rows, height, below(height), level, below(level))
        ]
        height = [
            h + f * (left_of(c) - c + a - r + g)
            for h, f, c, a, r, g in zip(
                height, factor, flux_cols, above(flux_rows), flux_rows, gain
            )
        ]
    return [h - b for h, b in zip(height, begin)]


def dot(a, b, dims):
    return lax.dot_general(
        a, b, (dims, ((), ())), precision=HIGHEST, preferred_element_type=jnp.float32
    )


def pivot_rows(pivot, rows):
    r0, r1, r2, r3 = rows
    p, q, s = pivot[0][0], pivot[0][1], pivot[1][1]
    inverse = 1.0 / (p * s - q * q)
    i00, i01, i11 = s * inverse, -q * inverse, p * inverse
    c0, c1, e0, e1 = pivot[0][2], pivot[1][2], pivot[0][3], pivot[1][3]
    y0, y1 = i00 * r0 + i01 * r1, i01 * r0 + i11 * r1
    f0, f1 = i00 * c0 + i01 * c1, i01 * c0 + i11 * c1
    g0, g1 = i00 * e0 + i01 * e1, i01 * e0 + i11 * e1
    s22 = pivot[2][2] - (c0 * f0 + c1 * f1)
    s23 = pivot[2][3] - (c0 * g0 + c1 * g1)
    s33 = pivot[3][3] - (e0 * g0 + e1 * g1)
    z2 = r2 - (c0 * y0 + c1 * y1)
    z3 = r3 - (e0 * y0 + e1 * y1)
    second = 1.0 / (s22 * s33 - s23 * s23)
    u2 = (s33 * z2 - s23 * z3) * second
    u3 = (s22 * z3 - s23 * z2) * second
    return [y0 - f0 * u2 - g0 * u3, y1 - f1 * u2 - g1 * u3, u2, u3]


def eliminate(gram, cross):
    size = gram.shape[0]
    work = jnp.concatenate([gram, cross], axis=1)
    width = work.shape[1]
    strips = [work[b : b + SUBLANES] for b in range(0, size, SUBLANES)]
    line = lax.broadcasted_iota(jnp.int32, (SUBLANES, width), 0)
    step = 4
    for k in range(0, size, step):
        columns = [
            [jnp.broadcast_to(s[:, k + i : k + i + 1], s.shape) for i in range(step)]
            for s in strips
        ]
        home, at = k // SUBLANES, k % SUBLANES
        rows = [strips[home][at + i : at + i + 1] for i in range(step)]
        pivot = [
            [columns[home][j][at + i : at + i + 1] for j in range(step)] for i in range(step)
        ]
        solved = pivot_rows(pivot, rows)
        following = []
        for b, s in enumerate(strips):
            c = columns[b]
            if b == home:
                for i in range(step):
                    s = jnp.where(line == at + i, solved[i], s)
                fixed = (line >= at) & (line < at + step)
                c = [jnp.where(fixed, 0.0, x) for x in c]
            s = s - ((c[0] * solved[0] + c[1] * solved[1]) + (c[2] * solved[2] + c[3] * solved[3]))
            following.append(s)
        strips = following
    return jnp.concatenate(strips, axis=0)[:, size:]


def mixing_of(predicted, innovation, error):
    members = predicted.shape[0]
    root = math.sqrt(members - 1.0)
    scaled = (predicted - jnp.mean(predicted, axis=0, keepdims=True)) / (error * root)
    both = dot(scaled, jnp.concatenate([scaled, innovation], axis=0), ((1,), (1,)))
    gram, cross = both[:, :members], both[:, members:]
    one = lax.broadcasted_iota(jnp.int32, gram.shape, 0)
    two = lax.broadcasted_iota(jnp.int32, gram.shape, 1)
    weights = eliminate(jnp.where(one == two, gram + INFLATION, gram), cross)
    return (weights - jnp.mean(weights, axis=0, keepdims=True)) / root


def local_kernel(
    count,
    perm_hbm,
    start_hbm,
    top_hbm,
    porosity_hbm,
    well_hbm,
    cells_hbm,
    observed_hbm,
    error_hbm,
    noise_hbm,
    first_own,
    patch_own,
    patch,
    mark,
    perm_ref,
    start_ref,
    top_ref,
    porosity_ref,
    well_ref,
    cells_ref,
    observed_ref,
    error_ref,
    noise_ref,
    stack,
    folded,
    load_sem,
):
    held, rows, cols = perm_ref.shape
    nobs = error_ref.shape[1]

    loads = [
        pltpu.make_async_copy(source, target, load_sem.at[index])
        for index, (source, target) in enumerate(
            [
                (perm_hbm, perm_ref),
                (start_hbm, start_ref),
                (top_hbm, top_ref),
                (porosity_hbm, porosity_ref),
                (well_hbm, well_ref),
                (cells_hbm, cells_ref),
                (observed_hbm, observed_ref),
                (error_hbm, error_ref),
                (noise_hbm, noise_ref),
            ]
        )
    ]
    for load in loads:
        load.start()

    for load in loads:
        load.wait()

    for strip in range(cols // LANES):
        part = slice(strip * LANES, (strip + 1) * LANES)
        fields = [perm_ref[member, :, part] for member in range(held)]
        fields += [start_ref[:, part], top_ref[:, part], porosity_ref[:, part]]
        fields += [well_ref[:, part].astype(jnp.float32)]
        for index, field in enumerate(fields):
            stack[strip, pl.ds(index, rows, stride=FIELDS), :] = field

    lane = lax.broadcasted_iota(jnp.int32, (QUARTERS * FIELDS, LANES), 1)
    quarter = lax.broadcasted_iota(jnp.int32, (QUARTERS * FIELDS, LANES), 0) // FIELDS
    flat = quarter * LANES + lane
    slot_of = (lane % HALF) // SIDE
    upper = lane < HALF

    def gather(chunk, cycle):
        total, marks = None, jnp.zeros(lane.shape, jnp.float32)
        for slot in range(SIDE):
            cell = cells_ref[cycle, chunk * SIDE + slot]
            row, col = lax.div(cell, cols), lax.rem(cell, cols)
            row0 = jnp.clip(row - STEPS, 0, rows - SIDE)
            col0 = jnp.clip(col - STEPS, 0, cols - SIDE)
            low = lax.div(col0, LANES)
            high = jnp.minimum(low + 1, cols // LANES - 1)
            within = col0 - low * LANES
            at = pl.multiple_of(row0 * FIELDS, FIELDS)
            left = stack[low, pl.ds(at, SIDE * FIELDS), :]
            right = stack[high, pl.ds(at, SIDE * FIELDS), :]
            inside = lane >= within
            here = quarter.shape[0]
            one = jnp.where(inside, left[:here], right[:here])
            two = jnp.where(inside, left[here:], right[here:])
            turn = lax.rem(slot * SIDE + LANES - within, LANES)
            one = pltpu.roll(one, turn, 1)
            two = pltpu.roll(two, lax.rem(turn + HALF, LANES), 1)
            moved = jnp.where(upper, one, two)
            total = moved if total is None else jnp.where(slot_of == slot, moved, total)
            down, along = row - row0, col - col0
            spot = lax.rem(down, QUARTERS) * LANES + lax.div(down, QUARTERS) * HALF
            marks = jnp.where(flat == spot + slot * SIDE + along, 1.0, marks)
        at = pl.ds(pl.multiple_of(chunk * (QUARTERS * FIELDS), FIELDS), QUARTERS * FIELDS)
        if cycle == 1:
            patch[at, :] = total
            mark[at, :] = marks
        return total, marks

    def first_chunk(chunk, carry):
        total, marks = gather(chunk, 0)
        parts = [total[v * FIELDS : (v + 1) * FIELDS] for v in range(QUARTERS)]
        marked = [marks[v * FIELDS : (v + 1) * FIELDS] for v in range(QUARTERS)]
        lines = [[p[held + f : held + f + 1] for p in parts] for f in range(4)]
        change = patch_plume(parts, *lines)
        sums = sum(jnp.where(m > 0.0, c, 0.0) for c, m in zip(change, marked))
        folded[pl.ds(pl.multiple_of(chunk * FIELDS, FIELDS), FIELDS), :] = sums
        return carry

    lax.fori_loop(0, count, first_chunk, 0, unroll=2)

    one = lax.broadcasted_iota(jnp.int32, (LANES, nobs), 0)
    two = lax.broadcasted_iota(jnp.int32, (LANES, nobs), 1)
    spread = dot(
        folded[...], jnp.where((one % HALF) // SIDE == two % SIDE, 1.0, 0.0), ((1,), (0,))
    ).reshape(count, FIELDS, nobs)
    turn = lax.broadcasted_iota(jnp.int32, spread.shape, 0)
    place = lax.broadcasted_iota(jnp.int32, spread.shape, 2)
    predicted = jnp.sum(jnp.where(place // SIDE == turn, spread, 0.0), axis=0)[:held]
    error = error_ref[...]
    first_own[0:held, :] = predicted
    first_own[held : 2 * held, :] = make_innovation(
        predicted, observed_ref[0:1, :], error, noise_ref[0]
    )
    first_own[2 * held : 3 * held, :] = make_innovation(
        jnp.zeros_like(predicted), observed_ref[1:2, :], error, noise_ref[1]
    )
    first_own[3 * held : 4 * held, :] = jnp.zeros_like(predicted)

    def second_chunk(chunk, carry):
        total, _ = gather(chunk, 1)
        for pair in range(QUARTERS // 2):
            at = 2 * pair * FIELDS
            patch_own[chunk, pair] = jnp.concatenate(
                [total[at : at + held], total[at + FIELDS : at + FIELDS + held]], axis=0
            )
        return carry

    lax.fori_loop(0, count, second_chunk, 0, unroll=2)


def ensemble_kernel(
    count,
    perm_ref,
    first_own,
    patch_own,
    patch,
    mark,
    error_ref,
    out_ref,
    first_all,
    patch_all,
    pred_all,
    block,
    mixed,
    send_sem,
    recv_sem,
    local_sem,
):
    held, rows, cols = perm_ref.shape
    members = held * count
    nobs = error_ref.shape[1]
    deep = count * FIELDS
    me = lax.axis_index("member")
    _, tall, wide = block.shape
    across = cols // wide

    def cells_of(ref, device):
        return ref.at[
            :,
            pl.ds(pl.multiple_of((device // across) * tall, tall), tall),
            pl.ds(pl.multiple_of((device % across) * wide, wide), wide),
        ]

    def members_of(ref, device):
        return ref.at[pl.ds(device * held, held)]

    def obs_of(ref, device):
        return ref.at[pl.ds(pl.multiple_of(device * SIDE, SIDE), SIDE)]

    ways = [
        (lambda peer: first_own, lambda owner: first_all.at[owner]),
        (lambda peer: patch_own.at[peer], lambda owner: patch_all.at[owner]),
        (lambda peer: cells_of(perm_ref, peer), lambda owner: members_of(block, owner)),
        (lambda peer: obs_of(pred_all, me), lambda owner: obs_of(pred_all, owner)),
        (lambda peer: members_of(mixed, peer), lambda owner: cells_of(out_ref, owner)),
    ]

    def transfer(kind, peer, owner, slot):
        source, target = ways[kind]
        return pltpu.make_async_remote_copy(
            src_ref=source(peer),
            dst_ref=target(owner),
            send_sem=send_sem.at[kind, slot],
            recv_sem=recv_sem.at[kind, slot],
            device_id={"member": peer},
            device_id_type=MESH,
        )

    def each(body, low=1, high=count):
        def step(j, carry):
            body(j)
            return carry

        lax.fori_loop(low, high, step, 0)

    def send(kind, low=1, high=count):
        each(lambda j: transfer(kind, lax.rem(me + j, count), me, j).start(), low, high)

    def receive(kind):
        each(lambda j: transfer(kind, me, lax.rem(me + count - j, count), j).wait_recv())

    def sent(kind):
        each(lambda j: transfer(kind, lax.rem(me + j, count), me, j).wait_send())

    barrier = pltpu.get_barrier_semaphore()
    each(
        lambda j: pl.semaphore_signal(
            barrier,
            inc=1,
            device_id={"member": lax.rem(me + j, count)},
            device_id_type=MESH,
        )
    )
    pl.semaphore_wait(barrier, count - 1)
    send(0)
    send(1)
    send(2)
    own_in = pltpu.make_async_copy(cells_of(perm_ref, me), members_of(block, me), local_sem.at[0])
    own_in.start()
    first_all[me] = first_own[...]
    patch_all[me] = patch_own[me]
    error = error_ref[...]

    depth = first_own.shape[0]
    line = lax.broadcasted_iota(jnp.int32, (members, count * depth), 0)
    spot = lax.broadcasted_iota(jnp.int32, (members, count * depth), 1)
    home = (line // held) * depth + line % held

    receive(0)
    whole = first_all[...].reshape(count * depth, nobs)

    def pick(offset):
        return dot(jnp.where(spot == home + offset, 1.0, 0.0), whole, ((1,), (0,)))

    first_mix = mixing_of(pick(0), pick(held), error)
    base = pick(2 * held)

    receive(1)
    line2 = lax.broadcasted_iota(jnp.int32, (members, deep), 0)
    spot2 = lax.broadcasted_iota(jnp.int32, (members, deep), 1)
    home2 = (line2 // held) * FIELDS + line2 % held
    at = pl.multiple_of(me * (QUARTERS * FIELDS), FIELDS)
    perms, lines, marked = [], [[], [], [], []], []
    for v in range(QUARTERS):
        choose = jnp.where(spot2 == home2 + (v % 2) * held, 1.0, 0.0)
        values = patch_all[:, v // 2].reshape(deep, LANES)
        prior = dot(choose, values, ((1,), (0,)))
        perms.append(prior + dot(first_mix, prior, ((0,), (0,))))
        own = patch[pl.ds(at + v * FIELDS, FIELDS), :]
        for f in range(4):
            lines[f].append(own[held + f : held + f + 1])
        marked.append(mark[pl.ds(at + v * FIELDS, FIELDS), :][0:1])
    change = patch_plume(perms, *lines)
    sums = sum(jnp.where(m > 0.0, c, 0.0) for c, m in zip(change, marked))
    one = lax.broadcasted_iota(jnp.int32, (SIDE, LANES), 0)
    two = lax.broadcasted_iota(jnp.int32, (SIDE, LANES), 1)
    fresh = dot(jnp.where((two % HALF) // SIDE == one, 1.0, 0.0), sums, ((1,), (1,)))
    pred_all[pl.ds(pl.multiple_of(me * SIDE, SIDE), SIDE), :] = jnp.concatenate(
        [fresh, jnp.zeros((SIDE, pred_all.shape[1] - members), jnp.float32)], axis=1
    )
    send(3)
    receive(3)
    table = pred_all[...].T[:members]
    second_mix = mixing_of(table, base - table / error, error)
    mixing = first_mix + second_mix + dot(first_mix, second_mix, ((1,), (0,)))

    receive(2)
    own_in.wait()
    for r in range(tall):
        prior = block[:, r, :]
        mixed[:, r, :] = prior + dot(mixing, prior, ((0,), (0,)))
    send(4)
    own_out = pltpu.make_async_copy(members_of(mixed, me), cells_of(out_ref, me), local_sem.at[1])
    own_out.start()
    for kind in range(4):
        sent(kind)
    own_out.wait()
    receive(4)
    sent(4)


def patch_device(count, perm, start, top, porosity, well, cells, observed, error, noise):
    held, rows, cols = perm.shape
    nobs = observed.shape[1]
    members = held * count
    wide = cols // ((count * SIDE) // rows)
    error = error.reshape(1, nobs)
    operands = (perm, start, top, porosity, well, cells, observed, error, noise)
    local = [
        (pltpu.SMEM if x is cells else pltpu.VMEM)(x.shape, x.dtype) for x in operands
    ]
    vmem = pl.BlockSpec(memory_space=pltpu.VMEM)
    grant = 32 * 1024 * 1024

    def scratch(*shape):
        return pltpu.VMEM(shape, jnp.float32)

    found = [
        (4 * held, nobs),
        (count, QUARTERS // 2, 2 * held, LANES),
        (count * QUARTERS * FIELDS, LANES),
        (count * QUARTERS * FIELDS, LANES),
    ]
    gathered = pl.pallas_call(
        functools.partial(local_kernel, count),
        out_shape=[jax.ShapeDtypeStruct(shape, jnp.float32) for shape in found],
        in_specs=[pl.BlockSpec(memory_space=pl.ANY)] * len(operands),
        out_specs=[vmem] * len(found),
        scratch_shapes=local
        + [
            scratch(cols // LANES, rows * FIELDS, LANES),
            scratch(count * FIELDS, LANES),
            pltpu.SemaphoreType.DMA((len(operands),)),
        ],
        compiler_params=pltpu.CompilerParams(vmem_limit_bytes=grant),
    )(*operands)
    return pl.pallas_call(
        functools.partial(ensemble_kernel, count),
        out_shape=jax.ShapeDtypeStruct(perm.shape, jnp.float32),
        in_specs=[vmem] * (len(found) + 2),
        out_specs=vmem,
        scratch_shapes=[
            scratch(count, *found[0]),
            scratch(*found[1]),
            scratch(nobs, LANES),
            scratch(members, SIDE, wide),
            scratch(members, SIDE, wide),
            pltpu.SemaphoreType.DMA((KINDS, count)),
            pltpu.SemaphoreType.DMA((KINDS, count)),
            pltpu.SemaphoreType.DMA((2,)),
        ],
        compiler_params=pltpu.CompilerParams(
            collective_id=0, has_side_effects=True, vmem_limit_bytes=grant
        ),
    )(perm, *gathered, error)


def fits(count, held, rows, cols, nobs):
    return (
        2 * held == FIELDS
        and 2 * count * held == LANES
        and nobs == LANES
        and nobs == count * SIDE
        and rows % SIDE == 0
        and (count * SIDE) % rows == 0
        and cols % ((count * SIDE // rows) * LANES) == 0
    )


def device_program(perm, *rest):
    count = lax.axis_size("member")
    held, rows, cols = perm.shape
    if fits(count, held, rows, cols, rest[5].shape[1]):
        return patch_device(count, perm, *rest)
    return on_device(perm, *rest)


def solution(mesh):
    return jax.shard_map(
        device_program,
        mesh=mesh,
        in_specs=(
            P(("region", "member"), None, None),
            P("region", None),
            P("region", None),
            P("region", None),
            P("region", None),
            P("region", None),
            P("region", None),
            P("region"),
            P("region", "member", None),
        ),
        out_specs=P(("region", "member"), None, None),
        check_vma=False,
    )
```

```python
import functools
import math

import jax
import jax.numpy as jnp
from jax import lax
from jax.experimental import pallas as pl
from jax.experimental.pallas import tpu as pltpu
from jax.sharding import PartitionSpec as P

MESH = pl.DeviceIdType.MESH
HIGHEST = lax.Precision.HIGHEST
SIDE = 8
LANES = 128
HALF = LANES // 2
QUARTERS = SIDE // 2
FIELDS = 8
SUBLANES = 8

STEPS = 3
CYCLES = 2


TIME_STEP = 0.01
INJECT_RATE = 1.0
INFLATION = 2.0
NOISE_CENTER = 127.5
NOISE_SPREAD = 73.9


def harmonic(first, second):
    return 2.0 * first * second / (first + second)


def plume_steps(perm_log, start_height, top_surface, porosity, well_mask):
    conduct = jnp.exp(perm_log)
    trans_rows = harmonic(conduct[:, :-1, :], conduct[:, 1:, :])
    trans_cols = harmonic(conduct[:, :, :-1], conduct[:, :, 1:])
    source = INJECT_RATE * well_mask.astype(jnp.float32)
    factor = TIME_STEP / porosity
    height = jnp.broadcast_to(start_height, perm_log.shape)
    for step_index in range(STEPS):
        level = height + top_surface
        flux_rows = (
            trans_rows
            * 0.5
            * (height[:, :-1, :] + height[:, 1:, :])
            * (level[:, :-1, :] - level[:, 1:, :])
        )
        flux_cols = (
            trans_cols
            * 0.5
            * (height[:, :, :-1] + height[:, :, 1:])
            * (level[:, :, :-1] - level[:, :, 1:])
        )
        inflow = jnp.pad(flux_rows, ((0, 0), (1, 0), (0, 0))) - jnp.pad(
            flux_rows, ((0, 0), (0, 1), (0, 0))
        )
        inflow = (
            inflow
            + jnp.pad(flux_cols, ((0, 0), (0, 0), (1, 0)))
            - jnp.pad(flux_cols, ((0, 0), (0, 0), (0, 1)))
        )
        height = height + factor * (inflow + source)
    return height


def make_innovation(predicted, observed, obs_error, noise):
    perturb = (noise.astype(jnp.float32) - NOISE_CENTER) / NOISE_SPREAD
    return (observed + math.sqrt(INFLATION) * obs_error * perturb - predicted) / obs_error


def gram_terms(predicted, innovation, obs_error):
    members = predicted.shape[0]
    scaled = (predicted - jnp.mean(predicted, axis=0, keepdims=True)) / (
        obs_error * math.sqrt(members - 1.0)
    )
    dims = (((1,), (1,)), ((), ()))
    gram = lax.dot_general(scaled, scaled, dims, precision=lax.Precision.HIGHEST)
    cross = lax.dot_general(scaled, innovation, dims, precision=lax.Precision.HIGHEST)
    return (gram, cross)


def solve_weights(gram, cross):
    members = gram.shape[0]
    full = gram + INFLATION * jnp.eye(members, dtype=jnp.float32)
    factor = jnp.linalg.cholesky(full)
    return jax.scipy.linalg.cho_solve((factor, True), cross)


def mix_fields(fields, weights):
    members = fields.shape[0]
    anomaly = (fields - jnp.mean(fields, axis=0, keepdims=True)) / math.sqrt(members - 1.0)
    return fields + lax.dot_general(
        weights, anomaly, (((0,), (0,)), ((), ())), precision=lax.Precision.HIGHEST
    )


def ensemble_solve(predicted, innovation, obs_error):
    whole_pred, whole_innov = (
        lax.all_gather(predicted, "member", axis=0, tiled=True),
        lax.all_gather(innovation, "member", axis=0, tiled=True),
    )
    gram, cross = gram_terms(whole_pred, whole_innov, obs_error)
    return solve_weights(gram, cross)


def on_device(
    perm_prior,
    start_height,
    top_surface,
    porosity,
    well_mask,
    obs_cells,
    observed,
    obs_error,
    noise_table,
):
    held_count, map_rows, map_cols = perm_prior.shape
    perm = perm_prior
    for cycle_index in range(CYCLES):
        height = plume_steps(perm, start_height, top_surface, porosity, well_mask)
        change = (height - start_height).reshape(held_count, map_rows * map_cols)
        predicted = jnp.take(change, obs_cells[cycle_index], axis=1)
        innovation = make_innovation(
            predicted, observed[cycle_index], obs_error, noise_table[cycle_index]
        )
        weights = ensemble_solve(predicted, innovation, obs_error)
        cell_major = lax.all_to_all(
            perm.reshape(held_count, map_rows * map_cols),
            "member",
            split_axis=1,
            concat_axis=0,
            tiled=True,
        )
        cell_major = mix_fields(cell_major, weights)
        returned = lax.all_to_all(cell_major, "member", split_axis=0, concat_axis=1, tiled=True)
        perm = returned.reshape(held_count, map_rows, map_cols)
    return perm


def patch_plume(perm_log, start, top, porosity, well):
    axis = perm_log[0].ndim - 1
    lane = lax.broadcasted_iota(jnp.int32, perm_log[0].shape, axis)
    inner_col = (lane % SIDE) < SIDE - 1
    upper = lane < HALF

    def right_of(x):
        return pltpu.roll(x, LANES - 1, axis)

    def left_of(x):
        return pltpu.roll(x, 1, axis)

    def below(xs):
        return xs[1:] + [pltpu.roll(xs[0], HALF, axis)]

    def above(xs):
        return [pltpu.roll(xs[-1], HALF, axis)] + xs[:-1]

    last = QUARTERS - 1
    conduct = [jnp.exp(p) for p in perm_log]
    half_cols = [jnp.where(inner_col, 0.5 * harmonic(c, right_of(c)), 0.0) for c in conduct]
    half_rows = [0.5 * harmonic(c, d) for c, d in zip(conduct, below(conduct))]
    half_rows[last] = jnp.where(upper, half_rows[last], 0.0)
    factor = [TIME_STEP / p for p in porosity]
    gain = [INJECT_RATE * w for w in well]
    begin = [jnp.broadcast_to(s, p.shape) for s, p in zip(start, perm_log)]
    height = begin
    for _ in range(STEPS):
        level = [h + t for h, t in zip(height, top)]
        flux_cols = [
            k * (h + right_of(h)) * (s - right_of(s))
            for k, h, s in zip(half_cols, height, level)
        ]
        flux_rows = [
            k * (h + g) * (s - r)
            for k, h, g, s, r in zip(half_rows, height, below(height), level, below(level))
        ]
        height = [
            h + f * (left_of(c) - c + a - r + g)
            for h, f, c, a, r, g in zip(
                height, factor, flux_cols, above(flux_rows), flux_rows, gain
            )
        ]
    return [h - b for h, b in zip(height, begin)]


def dot(a, b, dims):
    return lax.dot_general(
        a, b, (dims, ((), ())), precision=HIGHEST, preferred_element_type=jnp.float32
    )


def pivot_rows(pivot, rows):
    r0, r1, r2, r3 = rows
    p, q, s = pivot[0][0], pivot[0][1], pivot[1][1]
    inverse = 1.0 / (p * s - q * q)
    i00, i01, i11 = s * inverse, -q * inverse, p * inverse
    c0, c1, e0, e1 = pivot[0][2], pivot[1][2], pivot[0][3], pivot[1][3]
    y0, y1 = i00 * r0 + i01 * r1, i01 * r0 + i11 * r1
    f0, f1 = i00 * c0 + i01 * c1, i01 * c0 + i11 * c1
    g0, g1 = i00 * e0 + i01 * e1, i01 * e0 + i11 * e1
    s22 = pivot[2][2] - (c0 * f0 + c1 * f1)
    s23 = pivot[2][3] - (c0 * g0 + c1 * g1)
    s33 = pivot[3][3] - (e0 * g0 + e1 * g1)
    z2 = r2 - (c0 * y0 + c1 * y1)
    z3 = r3 - (e0 * y0 + e1 * y1)
    second = 1.0 / (s22 * s33 - s23 * s23)
    u2 = (s33 * z2 - s23 * z3) * second
    u3 = (s22 * z3 - s23 * z2) * second
    return [y0 - f0 * u2 - g0 * u3, y1 - f1 * u2 - g1 * u3, u2, u3]


def eliminate(gram, cross):
    size = gram.shape[0]
    work = jnp.concatenate([gram, cross], axis=1)
    width = work.shape[1]
    strips = [work[b : b + SUBLANES] for b in range(0, size, SUBLANES)]
    line = lax.broadcasted_iota(jnp.int32, (SUBLANES, width), 0)
    step = 4
    for k in range(0, size, step):
        columns = [
            [jnp.broadcast_to(s[:, k + i : k + i + 1], s.shape) for i in range(step)]
            for s in strips
        ]
        home, at = k // SUBLANES, k % SUBLANES
        rows = [strips[home][at + i : at + i + 1] for i in range(step)]
        pivot = [
            [columns[home][j][at + i : at + i + 1] for j in range(step)] for i in range(step)
        ]
        solved = pivot_rows(pivot, rows)
        following = []
        for b, s in enumerate(strips):
            c = columns[b]
            if b == home:
                for i in range(step):
                    s = jnp.where(line == at + i, solved[i], s)
                fixed = (line >= at) & (line < at + step)
                c = [jnp.where(fixed, 0.0, x) for x in c]
            s = s - ((c[0] * solved[0] + c[1] * solved[1]) + (c[2] * solved[2] + c[3] * solved[3]))
            following.append(s)
        strips = following
    return jnp.concatenate(strips, axis=0)[:, size:]


def mixing_of(predicted, innovation, error):
    members = predicted.shape[0]
    root = math.sqrt(members - 1.0)
    scaled = (predicted - jnp.mean(predicted, axis=0, keepdims=True)) / (error * root)
    both = dot(scaled, jnp.concatenate([scaled, innovation], axis=0), ((1,), (1,)))
    gram, cross = both[:, :members], both[:, members:]
    one = lax.broadcasted_iota(jnp.int32, gram.shape, 0)
    two = lax.broadcasted_iota(jnp.int32, gram.shape, 1)
    weights = eliminate(jnp.where(one == two, gram + INFLATION, gram), cross)
    return (weights - jnp.mean(weights, axis=0, keepdims=True)) / root


def local_kernel(
    count,
    perm_hbm,
    start_hbm,
    top_hbm,
    porosity_hbm,
    well_hbm,
    cells_hbm,
    patch_one,
    mark_one,
    patch_own,
    patch_two,
    mark_two,
    perm_ref,
    start_ref,
    top_ref,
    porosity_ref,
    well_ref,
    cells_ref,
    stack,
    patch_all_two,
    mark_all_two,
    load_sem,
):
    held, rows, cols = perm_ref.shape
    me = lax.axis_index("member")

    loads = [
        pltpu.make_async_copy(source, target, load_sem.at[index])
        for index, (source, target) in enumerate(
            [
                (perm_hbm, perm_ref),
                (start_hbm, start_ref),
                (top_hbm, top_ref),
                (porosity_hbm, porosity_ref),
                (well_hbm, well_ref),
                (cells_hbm, cells_ref),
            ]
        )
    ]
    for load in loads:
        load.start()

    for load in loads:
        load.wait()

    for strip in range(cols // LANES):
        part = slice(strip * LANES, (strip + 1) * LANES)
        fields = [perm_ref[member, :, part] for member in range(held)]
        fields += [start_ref[:, part], top_ref[:, part], porosity_ref[:, part]]
        fields += [well_ref[:, part].astype(jnp.float32)]
        for index, field in enumerate(fields):
            stack[strip, pl.ds(index, rows, stride=FIELDS), :] = field

    lane = lax.broadcasted_iota(jnp.int32, (SIDE * FIELDS, LANES), 1)
    short = (QUARTERS * FIELDS, LANES)
    low_lane = lax.broadcasted_iota(jnp.int32, short, 1)
    flat = lax.broadcasted_iota(jnp.int32, short, 0) // FIELDS * LANES + low_lane
    slot_of = lane // SIDE
    upper = low_lane < HALF
    cols_bits, lane_bits = cols.bit_length() - 1, LANES.bit_length() - 1

    def gather(chunk, cycle, patches, marked):
        total, marks = None, jnp.zeros(short, jnp.float32)
        for slot in range(SIDE):
            cell = cells_ref[cycle, chunk * SIDE + slot]
            row, col = cell >> cols_bits, cell & (cols - 1)
            row0 = jnp.clip(row - STEPS, 0, rows - SIDE)
            col0 = jnp.clip(col - STEPS, 0, cols - SIDE)
            low = col0 >> lane_bits
            high = jnp.minimum(low + 1, cols // LANES - 1)
            within = col0 & (LANES - 1)
            at = pl.multiple_of(row0 * FIELDS, FIELDS)
            left = stack[low, pl.ds(at, SIDE * FIELDS), :]
            right = stack[high, pl.ds(at, SIDE * FIELDS), :]
            window = jnp.where(lane >= within, left, right)
            moved = pltpu.roll(window, (slot * SIDE - within) & (LANES - 1), 1)
            total = moved if total is None else jnp.where(slot_of == slot, moved, total)
            down, along = row - row0, col - col0
            spot = (down & (QUARTERS - 1)) * LANES + (down // QUARTERS) * HALF + along
            marks = jnp.where(flat == spot + slot * SIDE, 1.0, marks)
        half = short[0]
        total = jnp.where(upper, total[:half], pltpu.roll(total[half:], HALF, 1))
        at = pl.ds(pl.multiple_of(chunk * half, FIELDS), half)
        patches[at, :] = total
        marked[at, :] = marks
        return total

    def first_chunk(chunk, carry):
        gather(chunk, 0, patch_one, mark_one)
        return carry

    def second_chunk(chunk, carry):
        total = gather(chunk, 1, patch_all_two, mark_all_two)
        rows_of = [total[v * FIELDS : v * FIELDS + held] for v in range(QUARTERS)]
        depth = QUARTERS * held
        at = pl.ds(pl.multiple_of(chunk * depth, FIELDS), depth)
        patch_own[at, :] = jnp.concatenate(rows_of, axis=0)
        return carry

    lax.fori_loop(0, count, second_chunk, 0, unroll=2)
    lax.fori_loop(0, count, first_chunk, 0, unroll=2)
    own = pl.ds(pl.multiple_of(me * short[0], FIELDS), short[0])
    patch_two[...] = patch_all_two[own, :]
    mark_two[...] = mark_all_two[own, :]


def ensemble_kernel(
    count,
    perm_ref,
    patch_one_hbm,
    mark_one_hbm,
    patch_own,
    patch_two_hbm,
    mark_two_hbm,
    observed_hbm,
    error_hbm,
    noise_hbm,
    out_ref,
    patch_one,
    mark_one,
    patch_two,
    mark_two,
    observed_ref,
    error_ref,
    noise_ref,
    folded,
    first_own,
    first_all,
    patch_all,
    pred_all,
    block,
    mixed,
    send_sem,
    recv_sem,
    load_sem,
):
    held, rows, cols = perm_ref.shape
    members = held * count
    nobs = error_ref.shape[1]
    depth = first_own.shape[0]
    me = lax.axis_index("member")
    tall, wide = block.shape[2:]
    across = cols // wide

    def cells_of(ref, device):
        return ref.at[
            :,
            pl.ds(pl.multiple_of((device // across) * tall, tall), tall),
            pl.ds(pl.multiple_of((device % across) * wide, wide), wide),
        ]

    def members_of(ref, device):
        return ref.at[:, device]

    def half_of(ref, device, half):
        return ref.at[
            :,
            pl.ds(pl.multiple_of((device // across) * tall, tall), tall),
            pl.ds(pl.multiple_of((device % across) * wide + half * LANES, LANES), LANES),
        ]

    def depth_of(ref, device):
        return ref.at[pl.ds(pl.multiple_of(device * depth, depth), depth)]

    def obs_of(ref, device):
        return ref.at[pl.ds(pl.multiple_of(device * SIDE, SIDE), SIDE)]

    ways = [
        (lambda peer: first_own, lambda owner: depth_of(first_all, owner)),
        (lambda peer: depth_of(patch_own, peer), lambda owner: depth_of(patch_all, owner)),
        (lambda peer: cells_of(perm_ref, peer), lambda owner: members_of(block, owner)),
        (lambda peer: obs_of(pred_all, me), lambda owner: obs_of(pred_all, owner)),
    ]
    for half in range(wide // LANES):
        ways.append(
            (
                lambda peer, half=half: members_of(mixed.at[half], peer),
                lambda owner, half=half: half_of(out_ref, owner, half),
            )
        )

    def transfer(kind, peer, owner, slot):
        source, target = ways[kind]
        return pltpu.make_async_remote_copy(
            src_ref=source(peer),
            dst_ref=target(owner),
            send_sem=send_sem.at[kind, slot],
            recv_sem=recv_sem.at[kind, slot],
            device_id={"member": peer},
            device_id_type=MESH,
        )

    def each(body, low=1, high=count):
        def step(j, carry):
            body(j)
            return carry

        lax.fori_loop(low, high, step, 0)

    def send(kind, low=1, high=count):
        each(lambda j: transfer(kind, lax.rem(me + j, count), me, j).start(), low, high)

    def receive(kind):
        each(lambda j: transfer(kind, me, lax.rem(me + count - j, count), j).wait_recv())

    def sent(kind):
        each(lambda j: transfer(kind, lax.rem(me + j, count), me, j).wait_send())

    loads = [
        pltpu.make_async_copy(source, target, load_sem.at[index])
        for index, (source, target) in enumerate(
            [
                (patch_one_hbm, patch_one),
                (mark_one_hbm, mark_one),
                (patch_two_hbm, patch_two),
                (mark_two_hbm, mark_two),
                (observed_hbm, observed_ref),
                (error_hbm, error_ref),
                (noise_hbm, noise_ref),
                (cells_of(perm_ref, me), members_of(block, me)),
                (depth_of(patch_own, me), depth_of(patch_all, me)),
            ]
        )
    ]
    for load in loads:
        load.start()

    barrier = pltpu.get_barrier_semaphore()
    each(
        lambda j: pl.semaphore_signal(
            barrier,
            inc=1,
            device_id={"member": lax.rem(me + j, count)},
            device_id_type=MESH,
        )
    )
    for load in loads:
        load.wait()
    pl.semaphore_wait(barrier, count - 1)
    third = (count + 1) // 3
    send(1)
    send(2, 1, third)

    group = QUARTERS * FIELDS

    def first_chunk(chunk, carry):
        at = pl.ds(pl.multiple_of(chunk * group, group), group)
        total, marks = patch_one[at, :], mark_one[at, :]
        parts = [total[v * FIELDS : (v + 1) * FIELDS] for v in range(QUARTERS)]
        marked = [marks[v * FIELDS : (v + 1) * FIELDS] for v in range(QUARTERS)]
        lines = [[p[held + f : held + f + 1] for p in parts] for f in range(4)]
        change = patch_plume(parts, *lines)
        sums = sum(jnp.where(m > 0.0, c, 0.0) for c, m in zip(change, marked))
        folded[pl.ds(pl.multiple_of(chunk * FIELDS, FIELDS), FIELDS), :] = sums
        return carry

    lax.fori_loop(0, count, first_chunk, 0, unroll=2)

    one = lax.broadcasted_iota(jnp.int32, (LANES, nobs), 0)
    two = lax.broadcasted_iota(jnp.int32, (LANES, nobs), 1)
    spread = dot(
        folded[...], jnp.where((one % HALF) // SIDE == two % SIDE, 1.0, 0.0), ((1,), (0,))
    ).reshape(count, FIELDS, nobs)
    turn = lax.broadcasted_iota(jnp.int32, spread.shape, 0)
    place = lax.broadcasted_iota(jnp.int32, spread.shape, 2)
    predicted = jnp.sum(jnp.where(place // SIDE == turn, spread, 0.0), axis=0)[:held]
    error = error_ref[...]
    first_own[0:held, :] = predicted
    first_own[held : 2 * held, :] = make_innovation(
        predicted, observed_ref[0:1, :], error, noise_ref[0]
    )
    first_own[2 * held : 3 * held, :] = make_innovation(
        jnp.zeros_like(predicted), observed_ref[1:2, :], error, noise_ref[1]
    )
    first_own[3 * held : 4 * held, :] = jnp.zeros_like(predicted)
    send(0)
    send(2, third, 2 * third)
    first_all[pl.ds(pl.multiple_of(me * depth, depth), depth), :] = first_own[...]

    def ordered(ref, offset):
        return jnp.concatenate(
            [ref[pl.ds(offset + m, count, stride=depth), :] for m in range(held)], axis=0
        )

    receive(0)
    send(2, 2 * third, count)
    first_mix = mixing_of(ordered(first_all, 0), ordered(first_all, held), error)
    base = ordered(first_all, 2 * held)

    receive(1)
    prior = jnp.concatenate([ordered(patch_all, v * held) for v in range(QUARTERS)], axis=1)
    shifted = prior + dot(first_mix, prior, ((0,), (0,)))
    perms, lines, marked = [], [[], [], [], []], []
    for v in range(QUARTERS):
        perms.append(shifted[:, v * LANES : (v + 1) * LANES])
        own = patch_two[v * FIELDS : (v + 1) * FIELDS, :]
        for f in range(4):
            lines[f].append(own[held + f : held + f + 1])
        marked.append(mark_two[v * FIELDS : v * FIELDS + 1, :])
    change = patch_plume(perms, *lines)
    sums = sum(jnp.where(m > 0.0, c, 0.0) for c, m in zip(change, marked))
    one = lax.broadcasted_iota(jnp.int32, (SIDE, LANES), 0)
    two = lax.broadcasted_iota(jnp.int32, (SIDE, LANES), 1)
    fresh = dot(jnp.where((two % HALF) // SIDE == one, 1.0, 0.0), sums, ((1,), (1,)))
    pred_all[pl.ds(pl.multiple_of(me * SIDE, SIDE), SIDE), :] = jnp.concatenate(
        [fresh, jnp.zeros((SIDE, pred_all.shape[1] - members), jnp.float32)], axis=1
    )
    send(3)
    receive(3)
    table = pred_all[...].T[:members]
    second_mix = mixing_of(table, base - table / error, error)
    mixing = first_mix + second_mix + dot(first_mix, second_mix, ((1,), (0,)))

    receive(2)
    for half in range(wide // LANES):
        part = slice(half * LANES, (half + 1) * LANES)
        for r in range(tall):
            prior = block[:, :, r, part].reshape(members, LANES)
            fresh = prior + dot(mixing, prior, ((0,), (0,)))
            mixed[half, :, :, r, :] = fresh.reshape(held, count, LANES)
        send(4 + half)
    own_out = [
        pltpu.make_async_copy(
            members_of(mixed.at[half], me), half_of(out_ref, me, half), load_sem.at[half]
        )
        for half in range(wide // LANES)
    ]
    for copy in own_out:
        copy.start()
    for kind in range(4):
        sent(kind)
    for copy in own_out:
        copy.wait()
    for half in range(wide // LANES):
        receive(4 + half)
        sent(4 + half)


def patch_device(count, perm, start, top, porosity, well, cells, observed, error, noise):
    held, rows, cols = perm.shape
    nobs = observed.shape[1]
    members = held * count
    wide = cols // ((count * SIDE) // rows)
    error = error.reshape(1, nobs)
    maps = (perm, start, top, porosity, well, cells)
    rest = (observed, error, noise)
    vmem = pl.BlockSpec(memory_space=pltpu.VMEM)
    anywhere = pl.BlockSpec(memory_space=pl.ANY)
    grant = 60 * 1024 * 1024
    depth = 4 * held
    group = QUARTERS * FIELDS
    kinds = 4 + wide // LANES

    def scratch(*shape):
        return pltpu.VMEM(shape, jnp.float32)

    found = [
        (count * group, LANES),
        (count * group, LANES),
        (count * depth, LANES),
        (group, LANES),
        (group, LANES),
    ]
    gathered = pl.pallas_call(
        functools.partial(local_kernel, count),
        out_shape=[jax.ShapeDtypeStruct(shape, jnp.float32) for shape in found],
        in_specs=[anywhere] * len(maps),
        out_specs=[vmem] * len(found),
        scratch_shapes=[pltpu.VMEM(x.shape, x.dtype) for x in maps[:-1]]
        + [
            pltpu.SMEM(cells.shape, cells.dtype),
            scratch(cols // LANES, rows * FIELDS, LANES),
            scratch(count * group, LANES),
            scratch(count * group, LANES),
            pltpu.SemaphoreType.DMA((len(maps),)),
        ],
        compiler_params=pltpu.CompilerParams(vmem_limit_bytes=grant),
    )(*maps)
    return pl.pallas_call(
        functools.partial(ensemble_kernel, count),
        out_shape=jax.ShapeDtypeStruct(perm.shape, jnp.float32),
        in_specs=[anywhere] * (1 + len(found) + len(rest)),
        out_specs=anywhere,
        scratch_shapes=[
            scratch(*found[0]),
            scratch(*found[1]),
            scratch(*found[3]),
            scratch(*found[4]),
        ]
        + [pltpu.VMEM(x.shape, x.dtype) for x in rest]
        + [
            scratch(count * FIELDS, LANES),
            scratch(depth, nobs),
            scratch(count * depth, nobs),
            scratch(count * depth, LANES),
            scratch(nobs, LANES),
            scratch(held, count, SIDE, wide),
            scratch(wide // LANES, held, count, SIDE, LANES),
            pltpu.SemaphoreType.DMA((kinds, count)),
            pltpu.SemaphoreType.DMA((kinds, count)),
            pltpu.SemaphoreType.DMA((len(found) + len(rest) + 1,)),
        ],
        compiler_params=pltpu.CompilerParams(
            collective_id=0, has_side_effects=True, vmem_limit_bytes=grant
        ),
    )(perm, *gathered, *rest)


def fits(count, held, rows, cols, nobs):
    return (
        2 * held == FIELDS
        and 2 * count * held == LANES
        and nobs == LANES
        and nobs == count * SIDE
        and rows % SIDE == 0
        and cols & (cols - 1) == 0
        and (count * SIDE) % rows == 0
        and cols % ((count * SIDE // rows) * LANES) == 0
    )


def device_program(perm, *rest):
    count = lax.axis_size("member")
    held, rows, cols = perm.shape
    if fits(count, held, rows, cols, rest[5].shape[1]):
        return patch_device(count, perm, *rest)
    return on_device(perm, *rest)


def solution(mesh):
    return jax.shard_map(
        device_program,
        mesh=mesh,
        in_specs=(
            P(("region", "member"), None, None),
            P("region", None),
            P("region", None),
            P("region", None),
            P("region", None),
            P("region", None),
            P("region", None),
            P("region"),
            P("region", "member", None),
        ),
        out_specs=P(("region", "member"), None, None),
        check_vma=False,
    )
```

```python
import functools
import math

import jax
import jax.numpy as jnp
from jax import lax
from jax.experimental import pallas as pl
from jax.experimental.pallas import tpu as pltpu
from jax.sharding import PartitionSpec as P

MESH = pl.DeviceIdType.MESH
HIGHEST = lax.Precision.HIGHEST
SIDE = 8
LANES = 128
HALF = LANES // 2
QUARTERS = SIDE // 2
FIELDS = 8
SUBLANES = 8

STEPS = 3
CYCLES = 2


TIME_STEP = 0.01
INJECT_RATE = 1.0
INFLATION = 2.0
NOISE_CENTER = 127.5
NOISE_SPREAD = 73.9


def harmonic(first, second):
    return 2.0 * first * second / (first + second)


def plume_steps(perm_log, start_height, top_surface, porosity, well_mask):
    conduct = jnp.exp(perm_log)
    trans_rows = harmonic(conduct[:, :-1, :], conduct[:, 1:, :])
    trans_cols = harmonic(conduct[:, :, :-1], conduct[:, :, 1:])
    source = INJECT_RATE * well_mask.astype(jnp.float32)
    factor = TIME_STEP / porosity
    height = jnp.broadcast_to(start_height, perm_log.shape)
    for step_index in range(STEPS):
        level = height + top_surface
        flux_rows = (
            trans_rows
            * 0.5
            * (height[:, :-1, :] + height[:, 1:, :])
            * (level[:, :-1, :] - level[:, 1:, :])
        )
        flux_cols = (
            trans_cols
            * 0.5
            * (height[:, :, :-1] + height[:, :, 1:])
            * (level[:, :, :-1] - level[:, :, 1:])
        )
        inflow = jnp.pad(flux_rows, ((0, 0), (1, 0), (0, 0))) - jnp.pad(
            flux_rows, ((0, 0), (0, 1), (0, 0))
        )
        inflow = (
            inflow
            + jnp.pad(flux_cols, ((0, 0), (0, 0), (1, 0)))
            - jnp.pad(flux_cols, ((0, 0), (0, 0), (0, 1)))
        )
        height = height + factor * (inflow + source)
    return height


def make_innovation(predicted, observed, obs_error, noise):
    perturb = (noise.astype(jnp.float32) - NOISE_CENTER) / NOISE_SPREAD
    return (observed + math.sqrt(INFLATION) * obs_error * perturb - predicted) / obs_error


def gram_terms(predicted, innovation, obs_error):
    members = predicted.shape[0]
    scaled = (predicted - jnp.mean(predicted, axis=0, keepdims=True)) / (
        obs_error * math.sqrt(members - 1.0)
    )
    dims = (((1,), (1,)), ((), ()))
    gram = lax.dot_general(scaled, scaled, dims, precision=lax.Precision.HIGHEST)
    cross = lax.dot_general(scaled, innovation, dims, precision=lax.Precision.HIGHEST)
    return (gram, cross)


def solve_weights(gram, cross):
    members = gram.shape[0]
    full = gram + INFLATION * jnp.eye(members, dtype=jnp.float32)
    factor = jnp.linalg.cholesky(full)
    return jax.scipy.linalg.cho_solve((factor, True), cross)


def mix_fields(fields, weights):
    members = fields.shape[0]
    anomaly = (fields - jnp.mean(fields, axis=0, keepdims=True)) / math.sqrt(members - 1.0)
    return fields + lax.dot_general(
        weights, anomaly, (((0,), (0,)), ((), ())), precision=lax.Precision.HIGHEST
    )


def ensemble_solve(predicted, innovation, obs_error):
    whole_pred, whole_innov = (
        lax.all_gather(predicted, "member", axis=0, tiled=True),
        lax.all_gather(innovation, "member", axis=0, tiled=True),
    )
    gram, cross = gram_terms(whole_pred, whole_innov, obs_error)
    return solve_weights(gram, cross)


def on_device(
    perm_prior,
    start_height,
    top_surface,
    porosity,
    well_mask,
    obs_cells,
    observed,
    obs_error,
    noise_table,
):
    held_count, map_rows, map_cols = perm_prior.shape
    perm = perm_prior
    for cycle_index in range(CYCLES):
        height = plume_steps(perm, start_height, top_surface, porosity, well_mask)
        change = (height - start_height).reshape(held_count, map_rows * map_cols)
        predicted = jnp.take(change, obs_cells[cycle_index], axis=1)
        innovation = make_innovation(
            predicted, observed[cycle_index], obs_error, noise_table[cycle_index]
        )
        weights = ensemble_solve(predicted, innovation, obs_error)
        cell_major = lax.all_to_all(
            perm.reshape(held_count, map_rows * map_cols),
            "member",
            split_axis=1,
            concat_axis=0,
            tiled=True,
        )
        cell_major = mix_fields(cell_major, weights)
        returned = lax.all_to_all(cell_major, "member", split_axis=0, concat_axis=1, tiled=True)
        perm = returned.reshape(held_count, map_rows, map_cols)
    return perm


def patch_plume(perm_log, start, top, porosity, well):
    axis = perm_log[0].ndim - 1
    lane = lax.broadcasted_iota(jnp.int32, perm_log[0].shape, axis)
    inner_col = (lane % SIDE) < SIDE - 1
    upper = lane < HALF

    def right_of(x):
        return pltpu.roll(x, LANES - 1, axis)

    def left_of(x):
        return pltpu.roll(x, 1, axis)

    def below(xs):
        return xs[1:] + [pltpu.roll(xs[0], HALF, axis)]

    def above(xs):
        return [pltpu.roll(xs[-1], HALF, axis)] + xs[:-1]

    last = QUARTERS - 1
    conduct = [jnp.exp(p) for p in perm_log]
    half_cols = [jnp.where(inner_col, 0.5 * harmonic(c, right_of(c)), 0.0) for c in conduct]
    half_rows = [0.5 * harmonic(c, d) for c, d in zip(conduct, below(conduct))]
    half_rows[last] = jnp.where(upper, half_rows[last], 0.0)
    factor = [TIME_STEP / p for p in porosity]
    gain = [INJECT_RATE * w for w in well]
    begin = [jnp.broadcast_to(s, p.shape) for s, p in zip(start, perm_log)]
    height = begin
    for _ in range(STEPS):
        level = [h + t for h, t in zip(height, top)]
        flux_cols = [
            k * (h + right_of(h)) * (s - right_of(s))
            for k, h, s in zip(half_cols, height, level)
        ]
        flux_rows = [
            k * (h + g) * (s - r)
            for k, h, g, s, r in zip(half_rows, height, below(height), level, below(level))
        ]
        height = [
            h + f * (left_of(c) - c + a - r + g)
            for h, f, c, a, r, g in zip(
                height, factor, flux_cols, above(flux_rows), flux_rows, gain
            )
        ]
    return [h - b for h, b in zip(height, begin)]


def dot(a, b, dims):
    return lax.dot_general(
        a, b, (dims, ((), ())), precision=HIGHEST, preferred_element_type=jnp.float32
    )


def pivot_rows(pivot, rows):
    r0, r1, r2, r3 = rows
    p, q, s = pivot[0][0], pivot[0][1], pivot[1][1]
    inverse = 1.0 / (p * s - q * q)
    i00, i01, i11 = s * inverse, -q * inverse, p * inverse
    c0, c1, e0, e1 = pivot[0][2], pivot[1][2], pivot[0][3], pivot[1][3]
    y0, y1 = i00 * r0 + i01 * r1, i01 * r0 + i11 * r1
    f0, f1 = i00 * c0 + i01 * c1, i01 * c0 + i11 * c1
    g0, g1 = i00 * e0 + i01 * e1, i01 * e0 + i11 * e1
    s22 = pivot[2][2] - (c0 * f0 + c1 * f1)
    s23 = pivot[2][3] - (c0 * g0 + c1 * g1)
    s33 = pivot[3][3] - (e0 * g0 + e1 * g1)
    z2 = r2 - (c0 * y0 + c1 * y1)
    z3 = r3 - (e0 * y0 + e1 * y1)
    second = 1.0 / (s22 * s33 - s23 * s23)
    u2 = (s33 * z2 - s23 * z3) * second
    u3 = (s22 * z3 - s23 * z2) * second
    return [y0 - f0 * u2 - g0 * u3, y1 - f1 * u2 - g1 * u3, u2, u3]


def eliminate(gram, cross):
    size = gram.shape[0]
    work = jnp.concatenate([gram, cross], axis=1)
    width = work.shape[1]
    strips = [work[b : b + SUBLANES] for b in range(0, size, SUBLANES)]
    line = lax.broadcasted_iota(jnp.int32, (SUBLANES, width), 0)
    step = 4
    for k in range(0, size, step):
        columns = [
            [jnp.broadcast_to(s[:, k + i : k + i + 1], s.shape) for i in range(step)]
            for s in strips
        ]
        home, at = k // SUBLANES, k % SUBLANES
        rows = [strips[home][at + i : at + i + 1] for i in range(step)]
        pivot = [
            [columns[home][j][at + i : at + i + 1] for j in range(step)] for i in range(step)
        ]
        solved = pivot_rows(pivot, rows)
        following = []
        for b, s in enumerate(strips):
            c = columns[b]
            if b == home:
                for i in range(step):
                    s = jnp.where(line == at + i, solved[i], s)
                fixed = (line >= at) & (line < at + step)
                c = [jnp.where(fixed, 0.0, x) for x in c]
            s = s - ((c[0] * solved[0] + c[1] * solved[1]) + (c[2] * solved[2] + c[3] * solved[3]))
            following.append(s)
        strips = following
    return jnp.concatenate(strips, axis=0)[:, size:]


def mixing_of(predicted, innovation, error):
    members = predicted.shape[0]
    root = math.sqrt(members - 1.0)
    scaled = (predicted - jnp.mean(predicted, axis=0, keepdims=True)) / (error * root)
    both = dot(scaled, jnp.concatenate([scaled, innovation], axis=0), ((1,), (1,)))
    gram, cross = both[:, :members], both[:, members:]
    one = lax.broadcasted_iota(jnp.int32, gram.shape, 0)
    two = lax.broadcasted_iota(jnp.int32, gram.shape, 1)
    weights = eliminate(jnp.where(one == two, gram + INFLATION, gram), cross)
    return (weights - jnp.mean(weights, axis=0, keepdims=True)) / root


def local_kernel(
    count,
    perm_hbm,
    start_hbm,
    top_hbm,
    porosity_hbm,
    well_hbm,
    cells_hbm,
    patch_one,
    mark_one,
    patch_own,
    patch_two,
    mark_two,
    perm_ref,
    start_ref,
    top_ref,
    porosity_ref,
    well_ref,
    cells_ref,
    stack,
    patch_all_two,
    mark_all_two,
    load_sem,
):
    held, rows, cols = perm_ref.shape
    me = lax.axis_index("member")

    loads = [
        pltpu.make_async_copy(source, target, load_sem.at[index])
        for index, (source, target) in enumerate(
            [
                (perm_hbm, perm_ref),
                (start_hbm, start_ref),
                (top_hbm, top_ref),
                (porosity_hbm, porosity_ref),
                (well_hbm, well_ref),
                (cells_hbm, cells_ref),
            ]
        )
    ]
    for load in loads:
        load.start()

    for load in loads:
        load.wait()

    for strip in range(cols // LANES):
        part = slice(strip * LANES, (strip + 1) * LANES)
        fields = [perm_ref[member, :, part] for member in range(held)]
        fields += [start_ref[:, part], top_ref[:, part], porosity_ref[:, part]]
        fields += [well_ref[:, part].astype(jnp.float32)]
        for index, field in enumerate(fields):
            stack[strip, pl.ds(index, rows, stride=FIELDS), :] = field

    lane = lax.broadcasted_iota(jnp.int32, (SIDE * FIELDS, LANES), 1)
    short = (QUARTERS * FIELDS, LANES)
    low_lane = lax.broadcasted_iota(jnp.int32, short, 1)
    flat = lax.broadcasted_iota(jnp.int32, short, 0) // FIELDS * LANES + low_lane
    slot_of = lane // SIDE
    upper = low_lane < HALF
    cols_bits, lane_bits = cols.bit_length() - 1, LANES.bit_length() - 1

    def gather(chunk, cycle, patches, marked):
        total, marks = None, jnp.zeros(short, jnp.float32)
        for slot in range(SIDE):
            cell = cells_ref[cycle, chunk * SIDE + slot]
            row, col = cell >> cols_bits, cell & (cols - 1)
            row0 = jnp.clip(row - STEPS, 0, rows - SIDE)
            col0 = jnp.clip(col - STEPS, 0, cols - SIDE)
            low = col0 >> lane_bits
            high = jnp.minimum(low + 1, cols // LANES - 1)
            within = col0 & (LANES - 1)
            at = pl.multiple_of(row0 * FIELDS, FIELDS)
            left = stack[low, pl.ds(at, SIDE * FIELDS), :]
            right = stack[high, pl.ds(at, SIDE * FIELDS), :]
            window = jnp.where(lane >= within, left, right)
            moved = pltpu.roll(window, (slot * SIDE - within) & (LANES - 1), 1)
            total = moved if total is None else jnp.where(slot_of == slot, moved, total)
            down, along = row - row0, col - col0
            spot = (down & (QUARTERS - 1)) * LANES + (down // QUARTERS) * HALF + along
            marks = jnp.where(flat == spot + slot * SIDE, 1.0, marks)
        half = short[0]
        total = jnp.where(upper, total[:half], pltpu.roll(total[half:], HALF, 1))
        at = pl.ds(pl.multiple_of(chunk * half, FIELDS), half)
        patches[at, :] = total
        marked[at, :] = marks
        return total

    def first_chunk(chunk, carry):
        gather(chunk, 0, patch_one, mark_one)
        return carry

    def second_chunk(chunk, carry):
        total = gather(chunk, 1, patch_all_two, mark_all_two)
        rows_of = [total[v * FIELDS : v * FIELDS + held] for v in range(QUARTERS)]
        depth = QUARTERS * held
        at = pl.ds(pl.multiple_of(chunk * depth, FIELDS), depth)
        patch_own[at, :] = jnp.concatenate(rows_of, axis=0)
        return carry

    lax.fori_loop(0, count, second_chunk, 0, unroll=4)
    lax.fori_loop(0, count, first_chunk, 0, unroll=4)
    own = pl.ds(pl.multiple_of(me * short[0], FIELDS), short[0])
    patch_two[...] = patch_all_two[own, :]
    mark_two[...] = mark_all_two[own, :]


def ensemble_kernel(
    count,
    perm_ref,
    patch_one_hbm,
    mark_one_hbm,
    patch_own,
    patch_two_hbm,
    mark_two_hbm,
    observed_hbm,
    error_hbm,
    noise_hbm,
    out_ref,
    patch_one,
    mark_one,
    patch_two,
    mark_two,
    observed_ref,
    error_ref,
    noise_ref,
    folded,
    first_own,
    first_all,
    patch_all,
    pred_all,
    block,
    mixed,
    send_sem,
    recv_sem,
    load_sem,
):
    held, rows, cols = perm_ref.shape
    members = held * count
    nobs = error_ref.shape[1]
    depth = first_own.shape[0]
    me = lax.axis_index("member")
    tall, wide = block.shape[2:]
    across = cols // wide

    def cells_of(ref, device):
        return ref.at[
            :,
            pl.ds(pl.multiple_of((device // across) * tall, tall), tall),
            pl.ds(pl.multiple_of((device % across) * wide, wide), wide),
        ]

    def members_of(ref, device):
        return ref.at[:, device]

    def half_of(ref, device, half):
        return ref.at[
            :,
            pl.ds(pl.multiple_of((device // across) * tall, tall), tall),
            pl.ds(pl.multiple_of((device % across) * wide + half * LANES, LANES), LANES),
        ]

    def depth_of(ref, device):
        return ref.at[pl.ds(pl.multiple_of(device * depth, depth), depth)]

    def obs_of(ref, device):
        return ref.at[pl.ds(pl.multiple_of(device * SIDE, SIDE), SIDE)]

    ways = [
        (lambda peer: first_own, lambda owner: depth_of(first_all, owner)),
        (lambda peer: depth_of(patch_own, peer), lambda owner: depth_of(patch_all, owner)),
        (lambda peer: cells_of(perm_ref, peer), lambda owner: members_of(block, owner)),
        (lambda peer: obs_of(pred_all, me), lambda owner: obs_of(pred_all, owner)),
    ]
    for half in range(wide // LANES):
        ways.append(
            (
                lambda peer, half=half: members_of(mixed.at[half], peer),
                lambda owner, half=half: half_of(out_ref, owner, half),
            )
        )

    def transfer(kind, peer, owner, slot):
        source, target = ways[kind]
        return pltpu.make_async_remote_copy(
            src_ref=source(peer),
            dst_ref=target(owner),
            send_sem=send_sem.at[kind, slot],
            recv_sem=recv_sem.at[kind, slot],
            device_id={"member": peer},
            device_id_type=MESH,
        )

    def each(body, low=1, high=count):
        def step(j, carry):
            body(j)
            return carry

        lax.fori_loop(low, high, step, 0)

    def send(kind, low=1, high=count):
        each(lambda j: transfer(kind, lax.rem(me + j, count), me, j).start(), low, high)

    def receive(kind):
        each(lambda j: transfer(kind, me, lax.rem(me + count - j, count), j).wait_recv())

    def sent(kind):
        each(lambda j: transfer(kind, lax.rem(me + j, count), me, j).wait_send())

    loads = [
        pltpu.make_async_copy(source, target, load_sem.at[index])
        for index, (source, target) in enumerate(
            [
                (patch_one_hbm, patch_one),
                (mark_one_hbm, mark_one),
                (patch_two_hbm, patch_two),
                (mark_two_hbm, mark_two),
                (observed_hbm, observed_ref),
                (error_hbm, error_ref),
                (noise_hbm, noise_ref),
                (cells_of(perm_ref, me), members_of(block, me)),
                (depth_of(patch_own, me), depth_of(patch_all, me)),
            ]
        )
    ]
    for load in loads:
        load.start()

    barrier = pltpu.get_barrier_semaphore()
    each(
        lambda j: pl.semaphore_signal(
            barrier,
            inc=1,
            device_id={"member": lax.rem(me + j, count)},
            device_id_type=MESH,
        )
    )
    for load in loads:
        load.wait()
    pl.semaphore_wait(barrier, count - 1)
    send(1)

    group = QUARTERS * FIELDS

    batch = min(8, count)

    def first_batch(index, carry):
        parts, lines, marked = [], [[], [], [], []], []
        for v in range(QUARTERS):
            totals, marks = [], []
            for i in range(batch):
                at = pl.multiple_of((index * batch + i) * group + v * FIELDS, FIELDS)
                totals.append(patch_one[pl.ds(at, FIELDS), :])
                marks.append(mark_one[pl.ds(at, FIELDS), :])
            parts.append(jnp.concatenate(totals, axis=0))
            marked.append(jnp.concatenate(marks, axis=0))
            for f in range(4):
                rows_of = [t[held + f : held + f + 1] for t in totals]
                spread = [jnp.broadcast_to(r, (FIELDS, LANES)) for r in rows_of]
                lines[f].append(jnp.concatenate(spread, axis=0))
        change = patch_plume(parts, *lines)
        sums = sum(jnp.where(m > 0.0, c, 0.0) for c, m in zip(change, marked))
        tall_batch = batch * FIELDS
        folded[pl.ds(pl.multiple_of(index * tall_batch, FIELDS), tall_batch), :] = sums
        return carry

    lax.fori_loop(0, count // batch, first_batch, 0)

    one = lax.broadcasted_iota(jnp.int32, (LANES, nobs), 0)
    two = lax.broadcasted_iota(jnp.int32, (LANES, nobs), 1)
    spread = dot(
        folded[...], jnp.where((one % HALF) // SIDE == two % SIDE, 1.0, 0.0), ((1,), (0,))
    ).reshape(count, FIELDS, nobs)
    turn = lax.broadcasted_iota(jnp.int32, spread.shape, 0)
    place = lax.broadcasted_iota(jnp.int32, spread.shape, 2)
    predicted = jnp.sum(jnp.where(place // SIDE == turn, spread, 0.0), axis=0)[:held]
    error = error_ref[...]
    first_own[0:held, :] = predicted
    first_own[held : 2 * held, :] = make_innovation(
        predicted, observed_ref[0:1, :], error, noise_ref[0]
    )
    first_own[2 * held : 3 * held, :] = make_innovation(
        jnp.zeros_like(predicted), observed_ref[1:2, :], error, noise_ref[1]
    )
    first_own[3 * held : 4 * held, :] = jnp.zeros_like(predicted)
    send(0)
    send(2)
    first_all[pl.ds(pl.multiple_of(me * depth, depth), depth), :] = first_own[...]

    def ordered(ref, offset):
        return jnp.concatenate(
            [ref[pl.ds(offset + m, count, stride=depth), :] for m in range(held)], axis=0
        )

    receive(0)
    first_mix = mixing_of(ordered(first_all, 0), ordered(first_all, held), error)
    base = ordered(first_all, 2 * held)

    receive(1)
    prior = jnp.concatenate([ordered(patch_all, v * held) for v in range(QUARTERS)], axis=1)
    shifted = prior + dot(first_mix, prior, ((0,), (0,)))
    perms, lines, marked = [], [[], [], [], []], []
    for v in range(QUARTERS):
        perms.append(shifted[:, v * LANES : (v + 1) * LANES])
        own = patch_two[v * FIELDS : (v + 1) * FIELDS, :]
        for f in range(4):
            lines[f].append(own[held + f : held + f + 1])
        marked.append(mark_two[v * FIELDS : v * FIELDS + 1, :])
    change = patch_plume(perms, *lines)
    sums = sum(jnp.where(m > 0.0, c, 0.0) for c, m in zip(change, marked))
    one = lax.broadcasted_iota(jnp.int32, (SIDE, LANES), 0)
    two = lax.broadcasted_iota(jnp.int32, (SIDE, LANES), 1)
    fresh = dot(jnp.where((two % HALF) // SIDE == one, 1.0, 0.0), sums, ((1,), (1,)))
    pred_all[pl.ds(pl.multiple_of(me * SIDE, SIDE), SIDE), :] = jnp.concatenate(
        [fresh, jnp.zeros((SIDE, pred_all.shape[1] - members), jnp.float32)], axis=1
    )
    send(3)
    receive(3)
    table = pred_all[...].T[:members]
    second_mix = mixing_of(table, base - table / error, error)
    mixing = first_mix + second_mix + dot(first_mix, second_mix, ((1,), (0,)))

    turned = mixing.T
    receive(2)
    for half in range(wide // LANES):
        part = slice(half * LANES, (half + 1) * LANES)
        for r in range(tall):
            prior = block[:, :, r, part].reshape(members, LANES)
            fresh = prior + dot(turned, prior, ((1,), (0,)))
            mixed[half, :, :, r, :] = fresh.reshape(held, count, LANES)
        send(4 + half)
    own_out = [
        pltpu.make_async_copy(
            members_of(mixed.at[half], me), half_of(out_ref, me, half), load_sem.at[half]
        )
        for half in range(wide // LANES)
    ]
    for copy in own_out:
        copy.start()
    for kind in range(4):
        sent(kind)
    for copy in own_out:
        copy.wait()
    for half in range(wide // LANES):
        receive(4 + half)
        sent(4 + half)


def patch_device(count, perm, start, top, porosity, well, cells, observed, error, noise):
    held, rows, cols = perm.shape
    nobs = observed.shape[1]
    members = held * count
    wide = cols // ((count * SIDE) // rows)
    error = error.reshape(1, nobs)
    maps = (perm, start, top, porosity, well, cells)
    rest = (observed, error, noise)
    vmem = pl.BlockSpec(memory_space=pltpu.VMEM)
    anywhere = pl.BlockSpec(memory_space=pl.ANY)
    grant = 60 * 1024 * 1024
    depth = 4 * held
    group = QUARTERS * FIELDS
    kinds = 4 + wide // LANES

    def scratch(*shape):
        return pltpu.VMEM(shape, jnp.float32)

    found = [
        (count * group, LANES),
        (count * group, LANES),
        (count * depth, LANES),
        (group, LANES),
        (group, LANES),
    ]
    gathered = pl.pallas_call(
        functools.partial(local_kernel, count),
        out_shape=[jax.ShapeDtypeStruct(shape, jnp.float32) for shape in found],
        in_specs=[anywhere] * len(maps),
        out_specs=[vmem] * len(found),
        scratch_shapes=[pltpu.VMEM(x.shape, x.dtype) for x in maps[:-1]]
        + [
            pltpu.SMEM(cells.shape, cells.dtype),
            scratch(cols // LANES, rows * FIELDS, LANES),
            scratch(count * group, LANES),
            scratch(count * group, LANES),
            pltpu.SemaphoreType.DMA((len(maps),)),
        ],
        compiler_params=pltpu.CompilerParams(vmem_limit_bytes=grant),
    )(*maps)
    return pl.pallas_call(
        functools.partial(ensemble_kernel, count),
        out_shape=jax.ShapeDtypeStruct(perm.shape, jnp.float32),
        in_specs=[anywhere] * (1 + len(found) + len(rest)),
        out_specs=anywhere,
        scratch_shapes=[
            scratch(*found[0]),
            scratch(*found[1]),
            scratch(*found[3]),
            scratch(*found[4]),
        ]
        + [pltpu.VMEM(x.shape, x.dtype) for x in rest]
        + [
            scratch(count * FIELDS, LANES),
            scratch(depth, nobs),
            scratch(count * depth, nobs),
            scratch(count * depth, LANES),
            scratch(nobs, LANES),
            scratch(held, count, SIDE, wide),
            scratch(wide // LANES, held, count, SIDE, LANES),
            pltpu.SemaphoreType.DMA((kinds, count)),
            pltpu.SemaphoreType.DMA((kinds, count)),
            pltpu.SemaphoreType.DMA((len(found) + len(rest) + 1,)),
        ],
        compiler_params=pltpu.CompilerParams(
            collective_id=0, has_side_effects=True, vmem_limit_bytes=grant
        ),
    )(perm, *gathered, *rest)


def fits(count, held, rows, cols, nobs):
    return (
        2 * held == FIELDS
        and 2 * count * held == LANES
        and nobs == LANES
        and nobs == count * SIDE
        and rows % SIDE == 0
        and cols & (cols - 1) == 0
        and count % min(8, count) == 0
        and (count * SIDE) % rows == 0
        and cols % ((count * SIDE // rows) * LANES) == 0
    )


def device_program(perm, *rest):
    count = lax.axis_size("member")
    held, rows, cols = perm.shape
    if fits(count, held, rows, cols, rest[5].shape[1]):
        return patch_device(count, perm, *rest)
    return on_device(perm, *rest)


def solution(mesh):
    return jax.shard_map(
        device_program,
        mesh=mesh,
        in_specs=(
            P(("region", "member"), None, None),
            P("region", None),
            P("region", None),
            P("region", None),
            P("region", None),
            P("region", None),
            P("region", None),
            P("region"),
            P("region", "member", None),
        ),
        out_specs=P(("region", "member"), None, None),
        check_vma=False,
    )
```

```python
import functools
import math

import jax
import jax.numpy as jnp
from jax import lax
from jax.experimental import pallas as pl
from jax.experimental.pallas import tpu as pltpu
from jax.sharding import PartitionSpec as P

MESH = pl.DeviceIdType.MESH
HIGHEST = lax.Precision.HIGHEST
SIDE = 8
LANES = 128
HALF = LANES // 2
QUARTERS = SIDE // 2
FIELDS = 8
SUBLANES = 8

STEPS = 3
CYCLES = 2


TIME_STEP = 0.01
INJECT_RATE = 1.0
INFLATION = 2.0
NOISE_CENTER = 127.5
NOISE_SPREAD = 73.9


def harmonic(first, second):
    return 2.0 * first * second / (first + second)


def plume_steps(perm_log, start_height, top_surface, porosity, well_mask):
    conduct = jnp.exp(perm_log)
    trans_rows = harmonic(conduct[:, :-1, :], conduct[:, 1:, :])
    trans_cols = harmonic(conduct[:, :, :-1], conduct[:, :, 1:])
    source = INJECT_RATE * well_mask.astype(jnp.float32)
    factor = TIME_STEP / porosity
    height = jnp.broadcast_to(start_height, perm_log.shape)
    for step_index in range(STEPS):
        level = height + top_surface
        flux_rows = (
            trans_rows
            * 0.5
            * (height[:, :-1, :] + height[:, 1:, :])
            * (level[:, :-1, :] - level[:, 1:, :])
        )
        flux_cols = (
            trans_cols
            * 0.5
            * (height[:, :, :-1] + height[:, :, 1:])
            * (level[:, :, :-1] - level[:, :, 1:])
        )
        inflow = jnp.pad(flux_rows, ((0, 0), (1, 0), (0, 0))) - jnp.pad(
            flux_rows, ((0, 0), (0, 1), (0, 0))
        )
        inflow = (
            inflow
            + jnp.pad(flux_cols, ((0, 0), (0, 0), (1, 0)))
            - jnp.pad(flux_cols, ((0, 0), (0, 0), (0, 1)))
        )
        height = height + factor * (inflow + source)
    return height


def make_innovation(predicted, observed, obs_error, noise):
    perturb = (noise.astype(jnp.float32) - NOISE_CENTER) / NOISE_SPREAD
    return (observed + math.sqrt(INFLATION) * obs_error * perturb - predicted) / obs_error


def gram_terms(predicted, innovation, obs_error):
    members = predicted.shape[0]
    scaled = (predicted - jnp.mean(predicted, axis=0, keepdims=True)) / (
        obs_error * math.sqrt(members - 1.0)
    )
    dims = (((1,), (1,)), ((), ()))
    gram = lax.dot_general(scaled, scaled, dims, precision=lax.Precision.HIGHEST)
    cross = lax.dot_general(scaled, innovation, dims, precision=lax.Precision.HIGHEST)
    return (gram, cross)


def solve_weights(gram, cross):
    members = gram.shape[0]
    full = gram + INFLATION * jnp.eye(members, dtype=jnp.float32)
    factor = jnp.linalg.cholesky(full)
    return jax.scipy.linalg.cho_solve((factor, True), cross)


def mix_fields(fields, weights):
    members = fields.shape[0]
    anomaly = (fields - jnp.mean(fields, axis=0, keepdims=True)) / math.sqrt(members - 1.0)
    return fields + lax.dot_general(
        weights, anomaly, (((0,), (0,)), ((), ())), precision=lax.Precision.HIGHEST
    )


def ensemble_solve(predicted, innovation, obs_error):
    whole_pred, whole_innov = (
        lax.all_gather(predicted, "member", axis=0, tiled=True),
        lax.all_gather(innovation, "member", axis=0, tiled=True),
    )
    gram, cross = gram_terms(whole_pred, whole_innov, obs_error)
    return solve_weights(gram, cross)


def on_device(
    perm_prior,
    start_height,
    top_surface,
    porosity,
    well_mask,
    obs_cells,
    observed,
    obs_error,
    noise_table,
):
    held_count, map_rows, map_cols = perm_prior.shape
    perm = perm_prior
    for cycle_index in range(CYCLES):
        height = plume_steps(perm, start_height, top_surface, porosity, well_mask)
        change = (height - start_height).reshape(held_count, map_rows * map_cols)
        predicted = jnp.take(change, obs_cells[cycle_index], axis=1)
        innovation = make_innovation(
            predicted, observed[cycle_index], obs_error, noise_table[cycle_index]
        )
        weights = ensemble_solve(predicted, innovation, obs_error)
        cell_major = lax.all_to_all(
            perm.reshape(held_count, map_rows * map_cols),
            "member",
            split_axis=1,
            concat_axis=0,
            tiled=True,
        )
        cell_major = mix_fields(cell_major, weights)
        returned = lax.all_to_all(cell_major, "member", split_axis=0, concat_axis=1, tiled=True)
        perm = returned.reshape(held_count, map_rows, map_cols)
    return perm


def patch_plume(perm_log, start, top, porosity, well):
    axis = perm_log[0].ndim - 1
    lane = lax.broadcasted_iota(jnp.int32, perm_log[0].shape, axis)
    inner_col = (lane % SIDE) < SIDE - 1
    upper = lane < HALF

    def right_of(x):
        return pltpu.roll(x, LANES - 1, axis)

    def left_of(x):
        return pltpu.roll(x, 1, axis)

    def below(xs):
        return xs[1:] + [pltpu.roll(xs[0], HALF, axis)]

    def above(xs):
        return [pltpu.roll(xs[-1], HALF, axis)] + xs[:-1]

    last = QUARTERS - 1
    conduct = [jnp.exp(p) for p in perm_log]
    half_cols = [jnp.where(inner_col, 0.5 * harmonic(c, right_of(c)), 0.0) for c in conduct]
    half_rows = [0.5 * harmonic(c, d) for c, d in zip(conduct, below(conduct))]
    half_rows[last] = jnp.where(upper, half_rows[last], 0.0)
    factor = [TIME_STEP / p for p in porosity]
    gain = [INJECT_RATE * w for w in well]
    begin = [jnp.broadcast_to(s, p.shape) for s, p in zip(start, perm_log)]
    height = begin
    for _ in range(STEPS):
        level = [h + t for h, t in zip(height, top)]
        flux_cols = [
            k * (h + right_of(h)) * (s - right_of(s))
            for k, h, s in zip(half_cols, height, level)
        ]
        flux_rows = [
            k * (h + g) * (s - r)
            for k, h, g, s, r in zip(half_rows, height, below(height), level, below(level))
        ]
        height = [
            h + f * (left_of(c) - c + a - r + g)
            for h, f, c, a, r, g in zip(
                height, factor, flux_cols, above(flux_rows), flux_rows, gain
            )
        ]
    return [h - b for h, b in zip(height, begin)]


def dot(a, b, dims):
    return lax.dot_general(
        a, b, (dims, ((), ())), precision=HIGHEST, preferred_element_type=jnp.float32
    )


def pivot_rows(pivot, rows):
    r0, r1, r2, r3 = rows
    p, q, s = pivot[0][0], pivot[0][1], pivot[1][1]
    inverse = 1.0 / (p * s - q * q)
    i00, i01, i11 = s * inverse, -q * inverse, p * inverse
    c0, c1, e0, e1 = pivot[0][2], pivot[1][2], pivot[0][3], pivot[1][3]
    y0, y1 = i00 * r0 + i01 * r1, i01 * r0 + i11 * r1
    f0, f1 = i00 * c0 + i01 * c1, i01 * c0 + i11 * c1
    g0, g1 = i00 * e0 + i01 * e1, i01 * e0 + i11 * e1
    s22 = pivot[2][2] - (c0 * f0 + c1 * f1)
    s23 = pivot[2][3] - (c0 * g0 + c1 * g1)
    s33 = pivot[3][3] - (e0 * g0 + e1 * g1)
    z2 = r2 - (c0 * y0 + c1 * y1)
    z3 = r3 - (e0 * y0 + e1 * y1)
    second = 1.0 / (s22 * s33 - s23 * s23)
    u2 = (s33 * z2 - s23 * z3) * second
    u3 = (s22 * z3 - s23 * z2) * second
    return [y0 - f0 * u2 - g0 * u3, y1 - f1 * u2 - g1 * u3, u2, u3]


def eliminate(gram, cross):
    size = gram.shape[0]
    work = jnp.concatenate([gram, cross], axis=1)
    width = work.shape[1]
    strips = [work[b : b + SUBLANES] for b in range(0, size, SUBLANES)]
    line = lax.broadcasted_iota(jnp.int32, (SUBLANES, width), 0)
    step = 4
    for k in range(0, size, step):
        columns = [
            [jnp.broadcast_to(s[:, k + i : k + i + 1], s.shape) for i in range(step)]
            for s in strips
        ]
        home, at = k // SUBLANES, k % SUBLANES
        rows = [strips[home][at + i : at + i + 1] for i in range(step)]
        pivot = [
            [columns[home][j][at + i : at + i + 1] for j in range(step)] for i in range(step)
        ]
        solved = pivot_rows(pivot, rows)
        following = []
        for b, s in enumerate(strips):
            c = columns[b]
            if b == home:
                for i in range(step):
                    s = jnp.where(line == at + i, solved[i], s)
                fixed = (line >= at) & (line < at + step)
                c = [jnp.where(fixed, 0.0, x) for x in c]
            s = s - ((c[0] * solved[0] + c[1] * solved[1]) + (c[2] * solved[2] + c[3] * solved[3]))
            following.append(s)
        strips = following
    return jnp.concatenate(strips, axis=0)[:, size:]


def mixing_of(predicted, innovation, error):
    members = predicted.shape[0]
    root = math.sqrt(members - 1.0)
    scaled = (predicted - jnp.mean(predicted, axis=0, keepdims=True)) / (error * root)
    both = dot(scaled, jnp.concatenate([scaled, innovation], axis=0), ((1,), (1,)))
    gram, cross = both[:, :members], both[:, members:]
    one = lax.broadcasted_iota(jnp.int32, gram.shape, 0)
    two = lax.broadcasted_iota(jnp.int32, gram.shape, 1)
    weights = eliminate(jnp.where(one == two, gram + INFLATION, gram), cross)
    return (weights - jnp.mean(weights, axis=0, keepdims=True)) / root


def local_kernel(
    count,
    perm_hbm,
    start_hbm,
    top_hbm,
    porosity_hbm,
    well_hbm,
    cells_hbm,
    patch_one,
    mark_one,
    patch_own,
    patch_two,
    mark_two,
    perm_ref,
    start_ref,
    top_ref,
    porosity_ref,
    well_ref,
    cells_ref,
    stack,
    patch_all_two,
    mark_all_two,
    load_sem,
):
    held, rows, cols = perm_ref.shape
    me = lax.axis_index("member")

    loads = [
        pltpu.make_async_copy(source, target, load_sem.at[index])
        for index, (source, target) in enumerate(
            [
                (perm_hbm, perm_ref),
                (start_hbm, start_ref),
                (top_hbm, top_ref),
                (porosity_hbm, porosity_ref),
                (well_hbm, well_ref),
                (cells_hbm, cells_ref),
            ]
        )
    ]
    for load in loads:
        load.start()

    for load in loads:
        load.wait()

    for strip in range(cols // LANES):
        part = slice(strip * LANES, (strip + 1) * LANES)
        fields = [perm_ref[member, :, part] for member in range(held)]
        fields += [start_ref[:, part], top_ref[:, part], porosity_ref[:, part]]
        fields += [well_ref[:, part].astype(jnp.float32)]
        for index, field in enumerate(fields):
            stack[strip, pl.ds(index, rows, stride=FIELDS), :] = field

    lane = lax.broadcasted_iota(jnp.int32, (SIDE * FIELDS, LANES), 1)
    short = (QUARTERS * FIELDS, LANES)
    low_lane = lax.broadcasted_iota(jnp.int32, short, 1)
    flat = lax.broadcasted_iota(jnp.int32, short, 0) // FIELDS * LANES + low_lane
    slot_of = lane // SIDE
    upper = low_lane < HALF
    cols_bits, lane_bits = cols.bit_length() - 1, LANES.bit_length() - 1

    def gather(chunk, cycle, patches, marked):
        total, marks = None, jnp.zeros(short, jnp.float32)
        for slot in range(SIDE):
            cell = cells_ref[cycle, chunk * SIDE + slot]
            row, col = cell >> cols_bits, cell & (cols - 1)
            row0 = jnp.clip(row - STEPS, 0, rows - SIDE)
            col0 = jnp.clip(col - STEPS, 0, cols - SIDE)
            low = col0 >> lane_bits
            high = jnp.minimum(low + 1, cols // LANES - 1)
            within = col0 & (LANES - 1)
            at = pl.multiple_of(row0 * FIELDS, FIELDS)
            left = stack[low, pl.ds(at, SIDE * FIELDS), :]
            right = stack[high, pl.ds(at, SIDE * FIELDS), :]
            window = jnp.where(lane >= within, left, right)
            moved = pltpu.roll(window, (slot * SIDE - within) & (LANES - 1), 1)
            total = moved if total is None else jnp.where(slot_of == slot, moved, total)
            down, along = row - row0, col - col0
            spot = (down & (QUARTERS - 1)) * LANES + (down // QUARTERS) * HALF + along
            marks = jnp.where(flat == spot + slot * SIDE, 1.0, marks)
        half = short[0]
        total = jnp.where(upper, total[:half], pltpu.roll(total[half:], HALF, 1))
        at = pl.ds(pl.multiple_of(chunk * half, FIELDS), half)
        patches[at, :] = total
        marked[at, :] = marks
        return total

    def first_chunk(chunk, carry):
        gather(chunk, 0, patch_one, mark_one)
        return carry

    def second_chunk(chunk, carry):
        total = gather(chunk, 1, patch_all_two, mark_all_two)
        rows_of = [total[v * FIELDS : v * FIELDS + held] for v in range(QUARTERS)]
        depth = QUARTERS * held
        at = pl.ds(pl.multiple_of(chunk * depth, FIELDS), depth)
        patch_own[at, :] = jnp.concatenate(rows_of, axis=0)
        return carry

    lax.fori_loop(0, count, second_chunk, 0, unroll=4)
    lax.fori_loop(0, count, first_chunk, 0, unroll=4)
    own = pl.ds(pl.multiple_of(me * short[0], FIELDS), short[0])
    patch_two[...] = patch_all_two[own, :]
    mark_two[...] = mark_all_two[own, :]


def ensemble_kernel(
    count,
    perm_ref,
    patch_one_hbm,
    mark_one_hbm,
    patch_own,
    patch_two_hbm,
    mark_two_hbm,
    observed_hbm,
    error_hbm,
    noise_hbm,
    out_ref,
    patch_one,
    mark_one,
    patch_two,
    mark_two,
    observed_ref,
    error_ref,
    noise_ref,
    folded,
    first_own,
    first_all,
    patch_all,
    pred_all,
    block,
    mixed,
    send_sem,
    recv_sem,
    load_sem,
):
    held, rows, cols = perm_ref.shape
    members = held * count
    nobs = error_ref.shape[1]
    depth = first_own.shape[0]
    me = lax.axis_index("member")
    tall, wide = block.shape[2:]
    across = cols // wide

    def cells_of(ref, device):
        return ref.at[
            :,
            pl.ds(pl.multiple_of((device // across) * tall, tall), tall),
            pl.ds(pl.multiple_of((device % across) * wide, wide), wide),
        ]

    def members_of(ref, device):
        return ref.at[:, device]

    def half_of(ref, device, half):
        return ref.at[
            :,
            pl.ds(pl.multiple_of((device // across) * tall, tall), tall),
            pl.ds(pl.multiple_of((device % across) * wide + half * LANES, LANES), LANES),
        ]

    def depth_of(ref, device):
        return ref.at[pl.ds(pl.multiple_of(device * depth, depth), depth)]

    def obs_of(ref, device):
        return ref.at[pl.ds(pl.multiple_of(device * SIDE, SIDE), SIDE)]

    ways = [
        (lambda peer: first_own, lambda owner: depth_of(first_all, owner)),
        (lambda peer: depth_of(patch_own, peer), lambda owner: depth_of(patch_all, owner)),
        (lambda peer: cells_of(perm_ref, peer), lambda owner: members_of(block, owner)),
        (lambda peer: obs_of(pred_all, me), lambda owner: obs_of(pred_all, owner)),
    ]
    for half in range(wide // LANES):
        ways.append(
            (
                lambda peer, half=half: members_of(mixed.at[half], peer),
                lambda owner, half=half: half_of(out_ref, owner, half),
            )
        )

    def transfer(kind, peer, owner, slot):
        source, target = ways[kind]
        return pltpu.make_async_remote_copy(
            src_ref=source(peer),
            dst_ref=target(owner),
            send_sem=send_sem.at[kind, slot],
            recv_sem=recv_sem.at[kind, slot],
            device_id={"member": peer},
            device_id_type=MESH,
        )

    def each(body, low=1, high=count):
        def step(j, carry):
            body(j)
            return carry

        lax.fori_loop(low, high, step, 0)

    def send(kind, low=1, high=count):
        def start(turn):
            by = (turn // 2) * (1 - 2 * (turn % 2))
            j = count // 2 + by
            transfer(kind, lax.rem(me + j, count), me, j).start()

        each(start, low, high)

    def receive(kind):
        each(lambda j: transfer(kind, me, lax.rem(me + count - j, count), j).wait_recv())

    def sent(kind):
        each(lambda j: transfer(kind, lax.rem(me + j, count), me, j).wait_send())

    loads = [
        pltpu.make_async_copy(source, target, load_sem.at[index])
        for index, (source, target) in enumerate(
            [
                (patch_one_hbm, patch_one),
                (mark_one_hbm, mark_one),
                (patch_two_hbm, patch_two),
                (mark_two_hbm, mark_two),
                (observed_hbm, observed_ref),
                (error_hbm, error_ref),
                (noise_hbm, noise_ref),
                (cells_of(perm_ref, me), members_of(block, me)),
                (depth_of(patch_own, me), depth_of(patch_all, me)),
            ]
        )
    ]
    for load in loads:
        load.start()

    barrier = pltpu.get_barrier_semaphore()
    each(
        lambda j: pl.semaphore_signal(
            barrier,
            inc=1,
            device_id={"member": lax.rem(me + j, count)},
            device_id_type=MESH,
        )
    )
    for load in loads:
        load.wait()
    pl.semaphore_wait(barrier, count - 1)
    send(1)
    send(2, 1, count // 4)

    group = QUARTERS * FIELDS

    batch = min(8, count)

    def first_batch(index, carry):
        parts, lines, marked = [], [[], [], [], []], []
        for v in range(QUARTERS):
            totals, marks = [], []
            for i in range(batch):
                at = pl.multiple_of((index * batch + i) * group + v * FIELDS, FIELDS)
                totals.append(patch_one[pl.ds(at, FIELDS), :])
                marks.append(mark_one[pl.ds(at, FIELDS), :])
            parts.append(jnp.concatenate(totals, axis=0))
            marked.append(jnp.concatenate(marks, axis=0))
            for f in range(4):
                rows_of = [t[held + f : held + f + 1] for t in totals]
                spread = [jnp.broadcast_to(r, (FIELDS, LANES)) for r in rows_of]
                lines[f].append(jnp.concatenate(spread, axis=0))
        change = patch_plume(parts, *lines)
        sums = sum(jnp.where(m > 0.0, c, 0.0) for c, m in zip(change, marked))
        tall_batch = batch * FIELDS
        folded[pl.ds(pl.multiple_of(index * tall_batch, FIELDS), tall_batch), :] = sums
        return carry

    lax.fori_loop(0, count // batch, first_batch, 0)

    one = lax.broadcasted_iota(jnp.int32, (LANES, nobs), 0)
    two = lax.broadcasted_iota(jnp.int32, (LANES, nobs), 1)
    spread = dot(
        folded[...], jnp.where((one % HALF) // SIDE == two % SIDE, 1.0, 0.0), ((1,), (0,))
    ).reshape(count, FIELDS, nobs)
    turn = lax.broadcasted_iota(jnp.int32, spread.shape, 0)
    place = lax.broadcasted_iota(jnp.int32, spread.shape, 2)
    predicted = jnp.sum(jnp.where(place // SIDE == turn, spread, 0.0), axis=0)[:held]
    error = error_ref[...]
    first_own[0:held, :] = predicted
    first_own[held : 2 * held, :] = make_innovation(
        predicted, observed_ref[0:1, :], error, noise_ref[0]
    )
    first_own[2 * held : 3 * held, :] = make_innovation(
        jnp.zeros_like(predicted), observed_ref[1:2, :], error, noise_ref[1]
    )
    first_own[3 * held : 4 * held, :] = jnp.zeros_like(predicted)
    send(0)
    send(2, count // 4, count)
    first_all[pl.ds(pl.multiple_of(me * depth, depth), depth), :] = first_own[...]

    def ordered(ref, offset):
        return jnp.concatenate(
            [ref[pl.ds(offset + m, count, stride=depth), :] for m in range(held)], axis=0
        )

    receive(0)
    first_mix = mixing_of(ordered(first_all, 0), ordered(first_all, held), error)
    base = ordered(first_all, 2 * held)

    receive(1)
    prior = jnp.concatenate([ordered(patch_all, v * held) for v in range(QUARTERS)], axis=1)
    shifted = prior + dot(first_mix, prior, ((0,), (0,)))
    perms, lines, marked = [], [[], [], [], []], []
    for v in range(QUARTERS):
        perms.append(shifted[:, v * LANES : (v + 1) * LANES])
        own = patch_two[v * FIELDS : (v + 1) * FIELDS, :]
        for f in range(4):
            lines[f].append(own[held + f : held + f + 1])
        marked.append(mark_two[v * FIELDS : v * FIELDS + 1, :])
    change = patch_plume(perms, *lines)
    sums = sum(jnp.where(m > 0.0, c, 0.0) for c, m in zip(change, marked))
    one = lax.broadcasted_iota(jnp.int32, (SIDE, LANES), 0)
    two = lax.broadcasted_iota(jnp.int32, (SIDE, LANES), 1)
    fresh = dot(jnp.where((two % HALF) // SIDE == one, 1.0, 0.0), sums, ((1,), (1,)))
    pred_all[pl.ds(pl.multiple_of(me * SIDE, SIDE), SIDE), :] = jnp.concatenate(
        [fresh, jnp.zeros((SIDE, pred_all.shape[1] - members), jnp.float32)], axis=1
    )
    send(3)
    receive(3)
    table = pred_all[...].T[:members]
    second_mix = mixing_of(table, base - table / error, error)
    mixing = first_mix + second_mix + dot(first_mix, second_mix, ((1,), (0,)))

    turned = mixing.T
    receive(2)
    for half in range(wide // LANES):
        part = slice(half * LANES, (half + 1) * LANES)
        for r in range(tall):
            prior = block[:, :, r, part].reshape(members, LANES)
            fresh = prior + dot(turned, prior, ((1,), (0,)))
            mixed[half, :, :, r, :] = fresh.reshape(held, count, LANES)
        send(4 + half)
    own_out = [
        pltpu.make_async_copy(
            members_of(mixed.at[half], me), half_of(out_ref, me, half), load_sem.at[half]
        )
        for half in range(wide // LANES)
    ]
    for copy in own_out:
        copy.start()
    for kind in range(4):
        sent(kind)
    for copy in own_out:
        copy.wait()
    for half in range(wide // LANES):
        receive(4 + half)
        sent(4 + half)


def patch_device(count, perm, start, top, porosity, well, cells, observed, error, noise):
    held, rows, cols = perm.shape
    nobs = observed.shape[1]
    members = held * count
    wide = cols // ((count * SIDE) // rows)
    error = error.reshape(1, nobs)
    maps = (perm, start, top, porosity, well, cells)
    rest = (observed, error, noise)
    vmem = pl.BlockSpec(memory_space=pltpu.VMEM)
    anywhere = pl.BlockSpec(memory_space=pl.ANY)
    grant = 60 * 1024 * 1024
    depth = 4 * held
    group = QUARTERS * FIELDS
    kinds = 4 + wide // LANES

    def scratch(*shape):
        return pltpu.VMEM(shape, jnp.float32)

    found = [
        (count * group, LANES),
        (count * group, LANES),
        (count * depth, LANES),
        (group, LANES),
        (group, LANES),
    ]
    gathered = pl.pallas_call(
        functools.partial(local_kernel, count),
        out_shape=[jax.ShapeDtypeStruct(shape, jnp.float32) for shape in found],
        in_specs=[anywhere] * len(maps),
        out_specs=[vmem] * len(found),
        scratch_shapes=[pltpu.VMEM(x.shape, x.dtype) for x in maps[:-1]]
        + [
            pltpu.SMEM(cells.shape, cells.dtype),
            scratch(cols // LANES, rows * FIELDS, LANES),
            scratch(count * group, LANES),
            scratch(count * group, LANES),
            pltpu.SemaphoreType.DMA((len(maps),)),
        ],
        compiler_params=pltpu.CompilerParams(vmem_limit_bytes=grant),
    )(*maps)
    return pl.pallas_call(
        functools.partial(ensemble_kernel, count),
        out_shape=jax.ShapeDtypeStruct(perm.shape, jnp.float32),
        in_specs=[anywhere] * (1 + len(found) + len(rest)),
        out_specs=anywhere,
        scratch_shapes=[
            scratch(*found[0]),
            scratch(*found[1]),
            scratch(*found[3]),
            scratch(*found[4]),
        ]
        + [pltpu.VMEM(x.shape, x.dtype) for x in rest]
        + [
            scratch(count * FIELDS, LANES),
            scratch(depth, nobs),
            scratch(count * depth, nobs),
            scratch(count * depth, LANES),
            scratch(nobs, LANES),
            scratch(held, count, SIDE, wide),
            scratch(wide // LANES, held, count, SIDE, LANES),
            pltpu.SemaphoreType.DMA((kinds, count)),
            pltpu.SemaphoreType.DMA((kinds, count)),
            pltpu.SemaphoreType.DMA((len(found) + len(rest) + 1,)),
        ],
        compiler_params=pltpu.CompilerParams(
            collective_id=0, has_side_effects=True, vmem_limit_bytes=grant
        ),
    )(perm, *gathered, *rest)


def fits(count, held, rows, cols, nobs):
    return (
        2 * held == FIELDS
        and 2 * count * held == LANES
        and nobs == LANES
        and nobs == count * SIDE
        and count % 4 == 0
        and rows % SIDE == 0
        and cols & (cols - 1) == 0
        and count % min(8, count) == 0
        and (count * SIDE) % rows == 0
        and cols % ((count * SIDE // rows) * LANES) == 0
    )


def device_program(perm, *rest):
    count = lax.axis_size("member")
    held, rows, cols = perm.shape
    if fits(count, held, rows, cols, rest[5].shape[1]):
        return patch_device(count, perm, *rest)
    return on_device(perm, *rest)


def solution(mesh):
    return jax.shard_map(
        device_program,
        mesh=mesh,
        in_specs=(
            P(("region", "member"), None, None),
            P("region", None),
            P("region", None),
            P("region", None),
            P("region", None),
            P("region", None),
            P("region", None),
            P("region"),
            P("region", "member", None),
        ),
        out_specs=P(("region", "member"), None, None),
        check_vma=False,
    )
```
